1024 devices in a mesh: section: 8 (over x_hi, y), expert: 32 (over z), copy: 4 (over x_lo, core).
Axes of the slice: x: 4 (x_hi: 2, x_lo: 2; x = x_hi * 2 + x_lo), y: 4, z: 32, core: 2. Of those that a mesh axis runs over, the one named last changes fastest.
Arguments:
- pending: bfloat16 [8, 4096, 4096], P('section', 'expert', 'copy'), may hold values from -6 to 6
- hidden: bfloat16 [8, 4096, 768], P('section', 'expert'), may hold values from -6 to 6
- logits: float32 [8, 4096, 4], P('section', 'expert')
- routes: int32 [8, 4096, 1], P('section', 'expert'), may hold values from 0 to 3; in each aligned block of 128 rows (0 to 127, 128 to 255, ..., all dimensions but the last counted through in order) at most 36 rows name the same one
- router_weight: float32 [8, 4096, 4], P('section', 'copy'), may hold values from -1.5 to 1.5
- down_weight: bfloat16 [8, 4, 768, 4096], P('section', 'copy', None, 'expert'), may hold values from -0.21875 to 0.21875
- master: float32 [8, 4, 768, 4096], P('section', 'copy', None, 'expert'), may hold values from -0.21875 to 0.21875
- moment_first: float32 [8, 4, 768, 4096], P('section', 'copy', None, 'expert'), may hold values from -64 to 64
- moment_second: float32 [8, 4, 768, 4096], P('section', 'copy', None, 'expert'), may hold values from 10 to 341
- push_plan: int32 [8, 4, 32, 96, 1], P('section', 'copy', 'expert'), may hold values from 0 to 31; in each aligned block of 96 rows (0 to 95, 96 to 191, ..., all dimensions but the last counted through in order) at most 5 rows name the same one
Outputs:
- input_grads: bfloat16 [8, 4096, 4096], P('section', 'expert', 'copy')
- master_out: float32 [8, 4, 768, 4096], P('section', 'copy', None, 'expert')
- moment_first_out: float32 [8, 4, 768, 4096], P('section', 'copy', None, 'expert')
- moment_second_out: float32 [8, 4, 768, 4096], P('section', 'copy', None, 'expert')
- serving: bfloat16 [8, 4, 32, 160, 8, 128], P('section', 'copy', 'expert')
The draws below stay inside these ranges and needn't reach their ends.
Inputs may be any that keep to these rules, and one draw needn't show every extreme that they name: `routes`: among the tokens of one index of expert, at most 36 are routed to any one expert. `push_plan`: among the blocks of one device, at most 5 go to any one owner.
All inputs are finite; a program needn't handle non-finite values.
Results may differ from the reference program's by a relative error of at most 0.0013.
Values may be sent and summed in bfloat16 or wider, within the bound.
A program may use at most 32 MiB of HBM per device.

```python
import math
import jax
import jax.numpy as jnp
import numpy as np
from jax import lax

D = 4096
FF_WIN = 768
TOK_DEV = 128
PUSH_ROWS = 8
EXPERTS = 4
DC = 1024
DW = 128
CAP = 36
TOKENS = 4096
PUSH_BLOCKS = 96
PUSH_MOST = 5
N_SECTION = 8
N_EXPERT = 32
N_COPY = 4


def draw_logits(key, part):
    key = jax.random.fold_in(key, 11)
    base_key = jax.random.fold_in(key, 0)
    values = 1.5 * jax.random.normal(base_key, (N_SECTION, TOKENS, EXPERTS), jnp.float32)
    return values


def shard_levels(rng, dims, pieces, least, largest):
    loudness, own = 1.0, jax.random.fold_in(rng, 6)
    for dim, shards_of in pieces:
        draws = jnp.exp(jax.random.uniform(jax.random.fold_in(own, dim), (shards_of,), jnp.float32, least / len(pieces), largest / len(pieces)))
        loudness = loudness * jnp.repeat(draws, dims[dim] // shards_of).reshape([-1 if axis == dim else 1 for axis in range(len(dims))])
    return loudness


def routed_block(own_key, own, number, rows, count, top, limit, skew):
    sequence = jax.random.permutation(own_key, count)
    crowded, ordinary = portions_of(count, rows * top, limit, skew, True), portions_of(count, rows * top, limit, skew, False)
    places = jnp.arange(count)

    def named(lengths, turn):
        used = int((lengths > 0).sum())
        fixed = max(1, used // 4)
        shifted = fixed + (places - fixed + turn * (used - fixed)) % max(1, count - fixed)
        return jnp.zeros((count,), jnp.int32).at[sequence[jnp.where(places < fixed, places, shifted)]].set(jnp.asarray(lengths, jnp.int32))

    lengths = jnp.where(number % 4 == 0, named(crowded, number // 4), named(ordinary, number - number // 4 - 1))
    mixed = jax.random.permutation(jax.random.fold_in(own, 3), count)
    giver, receiver = mixed[0:count // 2 * 2:2], mixed[1:count // 2 * 2:2]
    room = jnp.minimum(lengths[giver] - 1, limit - lengths[receiver]) // 2
    room = jnp.where((giver == sequence[0]) | (receiver == sequence[0]) | (lengths[receiver] == 0), 0, jnp.maximum(room, 0))
    shifted = jax.random.randint(jax.random.fold_in(own, 4), (count // 2,), 0, 1 << 20) % (room + 1)
    lengths = lengths.at[giver].add(-shifted).at[receiver].add(shifted)
    members = jnp.searchsorted(jnp.cumsum(lengths), jnp.arange(rows * top), side="right").astype(jnp.int32)
    listing = members.reshape(top, rows).T
    listing = listing[jax.random.permutation(jax.random.fold_in(own, 1), rows)]
    turn = jax.random.randint(jax.random.fold_in(own, 2), (rows, 1), 0, top)
    return jnp.take_along_axis(listing, (jnp.arange(top)[None, :] + turn) % top, axis=1)


def portions_of(count, total, reach, lean, full):
    portions = [(1 << 20) // math.isqrt(rank ** lean) + 1 for rank in range(1, count + 1)]
    largest = reach if full else min(reach, max(-(-total // count), total * portions[0] // sum(portions)))
    least = 1 if total - largest >= count - 1 else 0
    given, rest = [largest] + [least] * (count - 1), total - largest - least * (count - 1)
    while rest > 0:
        free = [i for i in range(1, count) if given[i] < largest] or [i for i in range(1, count) if given[i] < reach]
        whole, remaining = sum([portions[i] for i in free]), rest
        for i in free:
            extra = min(reach - given[i], max(1, remaining * portions[i] // whole), rest)
            given[i] = given[i] + extra
            rest = rest - extra
    return np.array(given)


def noise(rng, extent, scale, bound, cuts=(), kind=jnp.bfloat16):
    gain = shard_levels(rng, extent, cuts, -0.22, 0.18) if cuts else 1.0
    result = jax.random.normal(rng, extent, jnp.float32) * scale * gain
    return jnp.minimum(jnp.maximum(result, -bound), bound).astype(kind)


def setup_inputs(seed: int = 0) -> dict:
    key_of = jax.random.split(jax.random.key(seed), 11)
    pending = noise(key_of[0], (N_SECTION, TOKENS, D), 1.0, 6.0, ((0, 8), (1, 32), (2, 4)))
    hidden = noise(key_of[1], (N_SECTION, TOKENS, FF_WIN), 1.0, 6.0, ((0, 8), (1, 32)))
    logits = draw_logits(jax.random.fold_in(key_of[10], 71), 0)
    routes_keys = jax.random.split(jax.random.fold_in(key_of[3], 1), N_SECTION * TOKENS // TOK_DEV)
    routes_turns = jax.random.permutation(jax.random.fold_in(key_of[3], 3), N_SECTION * TOKENS // TOK_DEV)
    routes = jax.vmap(lambda own, number: routed_block(jax.random.fold_in(key_of[3], 2), own, number, TOK_DEV, EXPERTS, 1, CAP, 1))(routes_keys, routes_turns).reshape((N_SECTION, TOKENS, 1))
    router_weight = noise(key_of[4], (N_SECTION, D, EXPERTS), 0.1, 1.5, ((0, 8), (1, 4)), jnp.float32)
    down_weight = noise(key_of[5], (N_SECTION, N_COPY, FF_WIN, EXPERTS * DC), FF_WIN ** -0.5, 0.21875, ((0, 8), (1, 4), (3, 32)))
    master = noise(key_of[6], (N_SECTION, N_COPY, FF_WIN, EXPERTS * DC), FF_WIN ** -0.5, 0.21875, ((0, 8), (1, 4), (3, 32)), jnp.float32)
    moment_first = noise(key_of[7], (N_SECTION, N_COPY, FF_WIN, EXPERTS * DC), (max(1, TOKENS // (EXPERTS * 100))), 64.0, ((0, 8), (1, 4), (3, 32)), jnp.float32)
    moment_second = jnp.clip(jnp.exp(math.log(341.0) - 3.5292974 * jax.random.uniform(key_of[8], (N_SECTION, N_COPY, FF_WIN, EXPERTS * DC), jnp.float32) ** shard_levels(key_of[8], (N_SECTION, N_COPY, FF_WIN, EXPERTS * DC), ((0, 8), (1, 4), (3, 32)), -0.2, 0.2)), 10.0, 341.0)
    push_plan_keys = jax.random.split(jax.random.fold_in(key_of[9], 1), N_SECTION * N_COPY * N_EXPERT * PUSH_BLOCKS // PUSH_BLOCKS)
    push_plan_turns = jax.random.permutation(jax.random.fold_in(key_of[9], 3), N_SECTION * N_COPY * N_EXPERT * PUSH_BLOCKS // PUSH_BLOCKS)
    push_plan = jax.vmap(lambda own, number: routed_block(jax.random.fold_in(key_of[9], 2), own, number, PUSH_BLOCKS, N_EXPERT, 1, PUSH_MOST, 2))(push_plan_keys, push_plan_turns).reshape((N_SECTION, N_COPY, N_EXPERT, PUSH_BLOCKS, 1))
    return dict(pending=pending, hidden=hidden, logits=logits, routes=routes, router_weight=router_weight, down_weight=down_weight, master=master, moment_first=moment_first, moment_second=moment_second, push_plan=push_plan)


beta_first = 0.9
beta_second = 0.95
learn_rate = 0.002
decay_rate = 0.1
adam_eps = 1e-08
bias_first = 1.0 - 0.9 ** 10
bias_second = 1.0 - 0.95 ** 10

def section_backward(incoming, hidden_rows, logit_rows, route_ids, rweight, wdown):
    probability = jax.nn.softmax(logit_rows, axis=-1)
    expert_ids = jnp.arange(EXPERTS, dtype=jnp.int32)
    onehot = (route_ids[:, None] == expert_ids[None, :]).astype(jnp.float32)
    gate_value = lax.optimization_barrier(jnp.sum(probability * onehot, axis=-1))
    gate_half = gate_value.astype(jnp.bfloat16)
    scaled = (gate_half.astype(jnp.float32)[:, None] * incoming.astype(jnp.float32)).astype(jnp.bfloat16)
    row_limit = N_EXPERT * CAP

    def per_expert(expert):
        chosen = route_ids == expert
        position = jnp.nonzero(chosen, size=row_limit, fill_value=0)[0].astype(jnp.int32)
        validity = (jnp.arange(row_limit, dtype=jnp.int32) < jnp.sum(chosen.astype(jnp.int32))).astype(jnp.float32)
        weight = lax.dynamic_slice_in_dim(wdown, (expert * DC).astype(jnp.int32), DC, 2)
        weight = jnp.transpose(weight, (1, 0, 2)).reshape(FF_WIN, D)
        picked = hidden_rows[position]
        outputs = jnp.dot(picked, weight, preferred_element_type=jnp.float32)
        partial_value = lax.optimization_barrier(jnp.sum(outputs * incoming[position].astype(jnp.float32), axis=-1)) * validity
        gate_grad = jnp.zeros((TOKENS,), jnp.float32).at[position].add(partial_value)
        masked = scaled[position] * validity[:, None].astype(jnp.bfloat16)
        gradient = jnp.dot(picked.T, masked, preferred_element_type=jnp.float32)
        return (gate_grad, gradient.reshape(FF_WIN, N_COPY, DC))
    gate_grads, gradients = lax.map(per_expert, expert_ids)
    gate_grad = lax.optimization_barrier(jnp.sum(gate_grads, axis=0))
    logit_grad = (gate_grad * gate_value)[:, None] * (onehot - probability)
    router_term = jnp.dot(logit_grad, rweight.T, precision=lax.Precision.HIGHEST)
    input_grad = (incoming.astype(jnp.float32) + router_term).astype(jnp.bfloat16)
    gradient = jnp.transpose(gradients, (2, 1, 0, 3)).reshape(N_COPY, FF_WIN, EXPERTS * DC)
    return (input_grad, gradient)

def place_blocks(fresh_half, plan_ids):
    blocks = fresh_half.reshape(N_COPY, FF_WIN, N_EXPERT, DW).transpose(0, 2, 1, 3)
    blocks = blocks.reshape(N_COPY, N_EXPERT, PUSH_BLOCKS, PUSH_ROWS, DW)
    owners = plan_ids[..., 0]
    owner_hot = (owners[..., None] == jnp.arange(N_EXPERT, dtype=jnp.int32)).astype(jnp.int32)
    earlier = jnp.cumsum(owner_hot, axis=2) - owner_hot
    rank_ids = lax.optimization_barrier(jnp.sum(earlier * owner_hot, axis=-1))
    slot_ids = jnp.arange(N_EXPERT, dtype=jnp.int32)[None, :, None] * PUSH_MOST + rank_ids
    copy_ids = jnp.broadcast_to(jnp.arange(N_COPY, dtype=jnp.int32)[:, None, None], owners.shape)
    empty = jnp.zeros((N_COPY, N_EXPERT, N_EXPERT * PUSH_MOST, PUSH_ROWS, DW), jnp.bfloat16)
    return empty.at[copy_ids, owners, slot_ids].set(blocks)

def reference(pending, hidden, logits, routes, router_weight, down_weight, master, moment_first, moment_second, push_plan):
    grads_all = []
    masters = []
    firsts = []
    seconds = []
    servings = []
    for section_idx in range(N_SECTION):
        incoming = pending[(section_idx + 1) % N_SECTION]
        input_grad, gradient = section_backward(incoming, hidden[section_idx], logits[section_idx], routes[section_idx, :, 0], router_weight[section_idx], down_weight[section_idx])
        first_moment = beta_first * moment_first[section_idx] + (1.0 - beta_first) * gradient
        second_moment = beta_second * moment_second[section_idx] + (1.0 - beta_second) * gradient * gradient
        update = first_moment / bias_first / (jnp.sqrt(second_moment / bias_second) + adam_eps) + decay_rate * master[section_idx]
        fresh_master = master[section_idx] - learn_rate * update
        grads_all.append(input_grad)
        masters.append(fresh_master)
        firsts.append(first_moment)
        seconds.append(second_moment)
        servings.append(place_blocks(fresh_master.astype(jnp.bfloat16), push_plan[section_idx]))
    return (jnp.stack(grads_all), jnp.stack(masters), jnp.stack(firsts), jnp.stack(seconds), jnp.stack(servings))
```

```python
import functools

import jax
import jax.numpy as jnp
from jax import lax
from jax.experimental import pallas as pl
from jax.experimental.pallas import tpu as pltpu
from jax.sharding import PartitionSpec as P

PUSH_ROWS = 8
EXPERTS = 4
LANES = 128

beta_first = 0.9
beta_second = 0.95
learn_rate = 0.002
decay_rate = 0.1
adam_eps = 1e-08
bias_first = 1.0 - 0.9**10
bias_second = 1.0 - 0.95**10

F32 = jnp.float32
BF16 = jnp.bfloat16
I32 = jnp.int32
HIGHEST = lax.Precision.HIGHEST


def iota(shape, dim):
    return lax.broadcasted_iota(I32, shape, dim)


def mm(x, y, dims=((1,), (0,)), precision=None):
    return lax.dot_general(x, y, (dims, ((), ())), precision=precision, preferred_element_type=F32)


def kernel(
    n_sec, nz, slot_rows, gate_row,
    pend, hid, log_t, route_t, rw_t, w_hbm, ma_hbm, m1_hbm, m2_hbm, plan,
    ig_out, ma_out, m1_out, m2_out, serv,
    inc, hsend, hbuf, rsend, rbuf, scaled, gates, big, psend, ret_s, ret_r, cp_s, cp_r,
    wv, mav, m1v, m2v, fresh,
    ld_sem, st_sem, pend_sem, own_sem, ha_s, ha_r, zs, zr, xs, xr, cs, cr, rs, rr, ps, pr, gs, gr, ks, kr,
):
    grp = nz // EXPERTS
    cp = slot_rows
    tok = hid.shape[0]
    half = hid.shape[1] // 2
    ff = 2 * half
    s, z, c = lax.axis_index("section"), lax.axis_index("expert"), lax.axis_index("copy")
    a, b = c // 2, c % 2
    e, m = z // grp, z % grp
    here = (e // 2) * (2 * grp) + m * 2 + e % 2

    def place(p):
        q = p // grp
        return (q // 2) * (2 * grp) + (p % grp) * 2 + q % 2

    def remote(src, dst, send, recv, **axis):
        return pltpu.make_async_remote_copy(
            src_ref=src, dst_ref=dst, send_sem=send, recv_sem=recv,
            device_id=axis, device_id_type=pl.DeviceIdType.MESH,
        )

    loads = [
        pltpu.make_async_copy(src, dst, ld_sem.at[i])
        for i, (src, dst) in enumerate(((w_hbm, wv), (m1_hbm, m1v), (m2_hbm, m2v), (ma_hbm, mav)))
    ]
    for load in loads:
        load.start()

    barrier = pltpu.get_barrier_semaphore()
    prev_sec, next_sec = lax.rem(s + n_sec - 1, n_sec), lax.rem(s + 1, n_sec)

    def greet(**axis):
        pl.semaphore_signal(barrier, inc=1, device_id=axis, device_id_type=pl.DeviceIdType.MESH)

    greet(section=prev_sec)
    greet(section=next_sec)
    for k in range(1, 4):
        greet(copy=lax.rem(c + k, 4))

    @pl.loop(1, nz)
    def _(k):
        greet(expert=lax.rem(z + k, nz))

    pl.semaphore_wait(barrier, nz - 1 + 3 + 2)

    pend_copy = remote(pend, inc, pend_sem.at[0], pend_sem.at[1], section=prev_sec)
    pend_copy.start()

    logit = log_t[...]
    expd = jnp.exp(logit - jnp.max(logit, axis=0, keepdims=True))
    prob = expd / jnp.sum(expd, axis=0, keepdims=True)
    rid = route_t[...]
    onehot = (iota((EXPERTS, tok), 0) == rid).astype(F32)
    gate = jnp.sum(prob * onehot, axis=0, keepdims=True)
    hot8 = (iota((8, tok), 0) == rid).astype(F32)
    upper = (iota((tok, tok), 0) <= iota((tok, tok), 1)).astype(F32)
    running = mm(hot8.astype(BF16), upper.astype(BF16))
    rank = jnp.sum(running * hot8, axis=0, keepdims=True).astype(I32) - 1
    slot = rid * cp + rank
    placing = (iota((EXPERTS * cp, tok), 0) == slot).astype(F32).astype(BF16)
    gate8 = jnp.broadcast_to(gate, (8, tok)).astype(BF16)
    by_rank = []
    for x in range(EXPERTS):
        rank_x = jnp.where(rid == x, rank, -1)
        by_rank.append((iota((LANES, tok), 0) == rank_x).astype(F32))

    packed = mm(placing, hid[...]).astype(BF16)
    for x in range(EXPERTS):
        for h in range(2):
            hsend[h, x] = packed[x * cp:(x + 1) * cp, h * half:(h + 1) * half]

    def first_copy(d):
        other = lax.rem(e + d, EXPERTS)
        return remote(hsend.at[a, other], hbuf.at[a, b, m, e % 2], ha_s.at[d], ha_r.at[e % 2],
                      expert=other * grp + m)

    own_hidden = pltpu.make_async_copy(hsend.at[a, e], hbuf.at[a, b, m, e % 2], own_sem.at[0])

    @pl.when(b == e // 2)
    def _():
        for d in range(1, EXPERTS):
            first_copy(d).start()
        own_hidden.start()

    gate_rows = [
        mm(gate8, by_rank[x].astype(BF16), ((1,), (1,)))[0:1] for x in range(EXPERTS)
    ]

    pend_copy.wait_recv()
    for x in range(EXPERTS):
        rows = mm(placing[x * cp:(x + 1) * cp], inc[...])
        rid_rows = iota((cp, LANES), 0)
        for j in range(grp):
            piece = rows[:, j * LANES:(j + 1) * LANES]
            rsend[x * grp + j] = jnp.where(rid_rows >= gate_row, gate_rows[x], piece).astype(BF16)

    def row_copy(k):
        dest = lax.rem(z + k, nz)
        return remote(rsend.at[dest], rbuf.at[here], rs.at[k], rr.at[here], expert=dest)

    def row_arrival(k):
        src = lax.rem(z + k, nz)
        return remote(rsend.at[src], rbuf.at[place(src)], rs.at[k], rr.at[place(src)], expert=src)

    @pl.loop(1, nz // 2 + 1)
    def _(k):
        row_copy(k).start()

        @pl.when(k < nz // 2)
        def _():
            row_copy(nz - k).start()

    own_rows = pltpu.make_async_copy(rsend.at[z], rbuf.at[here], own_sem.at[1])
    own_rows.start()

    def chain_copy(block, way):
        return remote(hbuf.at[a, b, block], hbuf.at[a, b, block], zs.at[way, block], zr.at[block],
                      expert=lax.rem(z + (1 if way == 0 else nz - 1), nz))

    def x_copy(block, h):
        return remote(hbuf.at[h, b, block], hbuf.at[h, b, block], xs.at[block], xr.at[block],
                      copy=(1 - a) * 2 + b)

    def core_copy(block, h, kind, core):
        return remote(hbuf.at[h, core, block], hbuf.at[h, core, block], cs.at[kind, block],
                      cr.at[kind, block], copy=a * 2 + 1 - b)

    for i in range(2):
        @pl.when(2 * b + i != e)
        def _():
            remote(hsend.at[a, 0], hbuf.at[a, b, m, i], ha_s.at[0], ha_r.at[i], expert=m).wait_recv()

    @pl.when(b == e // 2)
    def _():
        own_hidden.wait()

    def spread(block):
        x_copy(block, a).start()
        core_copy(block, a, 0, b).start()

    @pl.when(m < grp - 1)
    def _():
        chain_copy(m, 0).start()

    @pl.when(m > 0)
    def _():
        chain_copy(m, 1).start()

    spread(m)

    @pl.loop(1, grp)
    def _(k):
        @pl.when(m - k >= 0)
        def _():
            chain_copy(m - k, 0).wait_recv()

            @pl.when(m < grp - 1)
            def _():
                chain_copy(m - k, 0).start()

            spread(m - k)

        @pl.when(m + k < grp)
        def _():
            chain_copy(m + k, 1).wait_recv()

            @pl.when(m > 0)
            def _():
                chain_copy(m + k, 1).start()

            spread(m + k)

    @pl.loop(0, grp)
    def _(block):
        x_copy(block, 1 - a).wait_recv()
        core_copy(block, 1 - a, 1, b).start()

    n_blocks = plan.shape[1]
    most = psend.shape[1] // PUSH_ROWS
    owner = plan[...]
    owner_hot = (iota((nz, n_blocks), 0) == owner).astype(F32)
    before = (iota((n_blocks, n_blocks), 0) < iota((n_blocks, n_blocks), 1)).astype(F32)
    earlier = mm(owner_hot.astype(BF16), before.astype(BF16))
    block_rank = jnp.sum(earlier * owner_hot, axis=0, keepdims=True)
    block_slot = jnp.broadcast_to(owner.astype(F32) * most + block_rank, (8, n_blocks))
    widen = (iota((n_blocks, ff), 1) // PUSH_ROWS == iota((n_blocks, ff), 0)).astype(F32)
    key = mm(block_slot.astype(BF16), widen.astype(BF16))[0:1].astype(I32)
    key = key * PUSH_ROWS + iota((1, ff), 1) % PUSH_ROWS
    big[...] = (iota((nz * most * PUSH_ROWS, ff), 0) == key).astype(F32).astype(BF16)

    for load in loads:
        load.wait()

    @pl.loop(0, grp)
    def _(block):
        core_copy(block, a, 0, 1 - b).wait_recv()
        core_copy(block, 1 - a, 1, 1 - b).wait_recv()

    own_rows.wait()

    @pl.loop(1, nz)
    def _(k):
        row_arrival(k).wait_recv()

    gates[...] = jnp.zeros(gates.shape, F32)
    for p in range(nz):
        gates[p:p + 1, :] = rbuf[p, 32:48, :].astype(F32)[gate_row - 32:gate_row - 31]
    gate_cols = gates[...].T
    for p in range(nz):
        scaled[p] = (gate_cols[0:cp, p:p + 1] * rbuf[p].astype(F32)).astype(BF16)
    scaled_all = scaled[...].reshape(nz * cp, LANES)
    for h in range(2):
        hidden_h = hbuf[h].reshape(nz * cp, half)
        grad = mm(scaled_all, hidden_h, ((0,), (0,))).T
        rows_h = pl.ds(h * half, half)
        first = beta_first * m1v[rows_h, :] + (1.0 - beta_first) * grad
        second = beta_second * m2v[rows_h, :] + (1.0 - beta_second) * grad * grad
        update = first / bias_first / (jnp.sqrt(second / bias_second) + adam_eps) + decay_rate * mav[rows_h, :]
        new = mav[rows_h, :] - learn_rate * update
        m1v[rows_h, :] = first
        m2v[rows_h, :] = second
        mav[rows_h, :] = new
        fresh[rows_h, :] = new.astype(BF16)
    per_owner = most * PUSH_ROWS
    for x in range(EXPERTS):
        part = mm(big[x * grp * per_owner:(x + 1) * grp * per_owner, :], fresh[...])
        for j in range(grp):
            psend[x * grp + j] = part[j * per_owner:(j + 1) * per_owner].astype(BF16)

    def push_copy(k):
        dest = lax.rem(z + k, nz)
        return remote(psend.at[dest], serv.at[z], ps.at[k], pr.at[z], expert=dest)

    def push_arrival(k):
        src = lax.rem(z + k, nz)
        return remote(psend.at[src], serv.at[src], ps.at[k], pr.at[src], expert=src)

    @pl.loop(1, nz // 2 + 1)
    def _(k):
        push_copy(k).start()

        @pl.when(k < nz // 2)
        def _():
            push_copy(nz - k).start()

    own_push = pltpu.make_async_copy(psend.at[z], serv.at[z], own_sem.at[2])
    own_push.start()
    stores = [
        pltpu.make_async_copy(src, dst, st_sem.at[i])
        for i, (src, dst) in enumerate(((m1v, m1_out), (m2v, m2_out), (mav, ma_out)))
    ]
    for store in stores:
        store.start()

    outputs = mm(hbuf[0].reshape(nz * cp, half), wv[0:half, :])
    outputs += mm(hbuf[1].reshape(nz * cp, half), wv[half:ff, :])
    product = outputs * rbuf[...].reshape(nz * cp, LANES).astype(F32)
    shares = mm(jnp.ones((8, LANES), F32), product, ((1,), (1,)), HIGHEST)
    for p in range(nz):
        ret_s[p, :, 0:cp] = shares[0:1, p * cp:(p + 1) * cp]

    def ret_copy(k):
        dest = lax.rem(z + k, nz)
        return remote(ret_s.at[place(dest)], ret_r.at[z], gs.at[k], gr.at[z], expert=dest)

    def ret_arrival(k):
        src = lax.rem(z + k, nz)
        return remote(ret_s.at[src], ret_r.at[src], gs.at[k], gr.at[src], expert=src)

    @pl.loop(1, nz // 2 + 1)
    def _(k):
        ret_copy(k).start()

        @pl.when(k < nz // 2)
        def _():
            ret_copy(nz - k).start()

    own_ret = pltpu.make_async_copy(ret_s.at[here], ret_r.at[z], own_sem.at[3])
    own_ret.start()
    own_ret.wait()

    @pl.loop(1, nz)
    def _(k):
        ret_arrival(k).wait_recv()

    for x in range(EXPERTS):
        total = ret_r[x * grp]
        for j in range(1, grp):
            total = total + ret_r[x * grp + j]
        cp_s[x:x + 1, :] = total

    def share_copy(k):
        return remote(cp_s, cp_r.at[k], ks.at[k], kr.at[k], copy=lax.rem(c + k, 4))

    for k in range(1, 4):
        share_copy(k).start()
    for k in range(1, 4):
        share_copy(k).wait_recv()
    whole = cp_s[...] + cp_r[1] + cp_r[2] + cp_r[3]
    whole = jnp.where(iota(whole.shape, 1) < cp, whole, 0.0)
    gate_grad = jnp.zeros((8, tok), F32)
    for x in range(EXPERTS):
        gate_grad += mm(jnp.broadcast_to(whole[x:x + 1], (8, LANES)), by_rank[x], precision=HIGHEST)
    logit_grad = (gate_grad[0:1] * gate) * (onehot - prob)
    gates[0:EXPERTS, :] = logit_grad
    grad_cols = gates[...].T
    term = inc[...].astype(F32)
    extra = grad_cols[:, 0:1] * rw_t[0:1, :]
    for x in range(1, EXPERTS):
        extra += grad_cols[:, x:x + 1] * rw_t[x:x + 1, :]
    ig_out[...] = (term + extra).astype(BF16)

    pend_copy.wait_send()
    for k in range(1, 4):
        share_copy(k).wait_send()

    @pl.when(b == e // 2)
    def _():
        for d in range(1, EXPERTS):
            first_copy(d).wait_send()

    @pl.loop(0, grp)
    def _(block):
        @pl.when((block <= m) & (m < grp - 1))
        def _():
            chain_copy(block, 0).wait_send()

        @pl.when((block >= m) & (m > 0))
        def _():
            chain_copy(block, 1).wait_send()

        x_copy(block, a).wait_send()
        core_copy(block, a, 0, b).wait_send()
        core_copy(block, 1 - a, 1, b).wait_send()

    @pl.loop(1, nz)
    def _(k):
        row_copy(k).wait_send()
        ret_copy(k).wait_send()

    for store in stores:
        store.wait()
    own_push.wait()

    @pl.loop(1, nz)
    def _(k):
        push_copy(k).wait_send()
        push_arrival(k).wait_recv()


def per_device(
    pending, hidden, logits, routes, router_weight, down_weight, master, moment_first, moment_second, push_plan,
):
    n_sec, nz = lax.axis_size("section"), lax.axis_size("expert")
    tok, width = pending.shape[1:]
    ff = hidden.shape[2]
    grp = nz // EXPERTS
    capacity = tok * 9 // (EXPERTS * 8)
    cp = 48
    gate_row = 40
    n_blocks = ff // PUSH_ROWS
    most = max(2, (3 * n_blocks + 2 * nz - 1) // (2 * nz))
    assert capacity <= gate_row and width == grp * LANES and tok == LANES
    per_owner = most * PUSH_ROWS
    half = ff // 2
    vmem, hbm = pl.BlockSpec(memory_space=pltpu.VMEM), pl.BlockSpec(memory_space=pl.ANY)
    dma = pltpu.SemaphoreType.DMA
    piece = jax.ShapeDtypeStruct((ff, LANES), F32)
    input_grad, fresh_master, first, second, serving = pl.pallas_call(
        functools.partial(kernel, n_sec, nz, cp, gate_row),
        out_shape=(
            jax.ShapeDtypeStruct((tok, width), BF16), piece, piece, piece,
            jax.ShapeDtypeStruct((nz, per_owner, LANES), BF16),
        ),
        in_specs=[hbm] + [vmem] * 4 + [hbm] * 4 + [vmem],
        out_specs=[vmem] + [hbm] * 4,
        scratch_shapes=[
            pltpu.VMEM((tok, width), BF16),
            pltpu.VMEM((2, EXPERTS, cp, half), BF16),
            pltpu.VMEM((2, 2, grp, 2, cp, half), BF16),
            pltpu.VMEM((nz, cp, LANES), BF16),
            pltpu.VMEM((nz, cp, LANES), BF16),
            pltpu.VMEM((nz, cp, LANES), BF16),
            pltpu.VMEM((LANES, LANES), F32),
            pltpu.VMEM((nz * per_owner, ff), BF16),
            pltpu.VMEM((nz, per_owner, LANES), BF16),
            pltpu.VMEM((nz, 1, LANES), F32),
            pltpu.VMEM((nz, 1, LANES), F32),
            pltpu.VMEM((EXPERTS, LANES), F32),
            pltpu.VMEM((4, EXPERTS, LANES), F32),
            pltpu.VMEM((ff, LANES), BF16),
            pltpu.VMEM((ff, LANES), F32),
            pltpu.VMEM((ff, LANES), F32),
            pltpu.VMEM((ff, LANES), F32),
            pltpu.VMEM((ff, LANES), BF16),
            dma((4,)), dma((3,)), dma((2,)), dma((4,)),
            dma((EXPERTS,)), dma((2,)),
            dma((2, grp)), dma((grp,)),
            dma((grp,)), dma((grp,)),
            dma((2, grp)), dma((2, grp)),
            dma((nz,)), dma((nz,)),
            dma((nz,)), dma((nz,)),
            dma((nz,)), dma((nz,)),
            dma((4,)), dma((4,)),
        ],
        compiler_params=pltpu.CompilerParams(
            collective_id=0, has_side_effects=True, vmem_limit_bytes=48 * 1024 * 1024
        ),
        cost_estimate=pl.CostEstimate(flops=10**9, bytes_accessed=8 * 10**6, transcendentals=10**5),
    )(
        pending[0], hidden[0], logits[0].T, routes[0].T, router_weight[0].T,
        down_weight[0, 0], master[0, 0], moment_first[0, 0], moment_second[0, 0], push_plan[0, 0, 0].T,
    )
    return (
        input_grad[None],
        fresh_master[None, None],
        first[None, None],
        second[None, None],
        serving.reshape(nz * most, PUSH_ROWS, LANES)[None, None, None],
    )


def solution(mesh):
    return jax.shard_map(
        per_device,
        mesh=mesh,
        in_specs=(
            P("section", "expert", "copy"),
            P("section", "expert", None),
            P("section", "expert", None),
            P("section", "expert", None),
            P("section", "copy", None),
            P("section", "copy", None, "expert"),
            P("section", "copy", None, "expert"),
            P("section", "copy", None, "expert"),
            P("section", "copy", None, "expert"),
            P("section", "copy", "expert", None, None),
        ),
        out_specs=(
            P("section", "expert", "copy"),
            P("section", "copy", None, "expert"),
            P("section", "copy", None, "expert"),
            P("section", "copy", None, "expert"),
            P("section", "copy", "expert", None, None, None),
        ),
        check_vma=False,
    )
```

```python
import functools

import jax
import jax.numpy as jnp
from jax import lax
from jax.experimental import pallas as pl
from jax.experimental.pallas import tpu as pltpu
from jax.sharding import PartitionSpec as P

PUSH_ROWS = 8
EXPERTS = 4
LANES = 128

beta_first = 0.9
beta_second = 0.95
learn_rate = 0.002
decay_rate = 0.1
adam_eps = 1e-08
bias_first = 1.0 - 0.9**10
bias_second = 1.0 - 0.95**10

F32 = jnp.float32
BF16 = jnp.bfloat16
I32 = jnp.int32
HIGHEST = lax.Precision.HIGHEST


def iota(shape, dim):
    return lax.broadcasted_iota(I32, shape, dim)


def mm(x, y, dims=((1,), (0,)), precision=None):
    return lax.dot_general(x, y, (dims, ((), ())), precision=precision, preferred_element_type=F32)


def kernel(
    n_sec, nz, slot_rows, gate_row,
    pend, hid, log_t, route_t, rw_t, w_hbm, ma_hbm, m1_hbm, m2_hbm, plan,
    ig_out, ma_out, m1_out, m2_out, serv,
    inc, hsend, hbuf, hflat, rsend, rbuf, scaled, gates, big, psend, ret_s, ret_r, cp_s, cp_r,
    wv, mav, m1v, m2v, fresh,
    ld_sem, st_sem, pend_sem, own_sem, ha_s, ha_r, zs, zr, xs, xr, cs, cr, rs, rr, ps, pr, gs, gr, ks, kr,
):
    grp = nz // EXPERTS
    cp = slot_rows
    tok = hid.shape[0]
    half = hid.shape[1] // 2
    ff = 2 * half
    s, z, c = lax.axis_index("section"), lax.axis_index("expert"), lax.axis_index("copy")
    a, b = c // 2, c % 2
    e, m = z // grp, z % grp
    here = (e // 2) * (2 * grp) + m * 2 + e % 2

    def place(p):
        q = p // grp
        return (q // 2) * (2 * grp) + (p % grp) * 2 + q % 2

    def remote(src, dst, send, recv, **axis):
        return pltpu.make_async_remote_copy(
            src_ref=src, dst_ref=dst, send_sem=send, recv_sem=recv,
            device_id=axis, device_id_type=pl.DeviceIdType.MESH,
        )

    loads = [
        pltpu.make_async_copy(src, dst, ld_sem.at[i])
        for i, (src, dst) in enumerate(((w_hbm, wv), (m1_hbm, m1v), (m2_hbm, m2v), (ma_hbm, mav)))
    ]
    for load in loads:
        load.start()

    barrier = pltpu.get_barrier_semaphore()
    prev_sec, next_sec = lax.rem(s + n_sec - 1, n_sec), lax.rem(s + 1, n_sec)

    def greet(**axis):
        pl.semaphore_signal(barrier, inc=1, device_id=axis, device_id_type=pl.DeviceIdType.MESH)

    greet(section=prev_sec)
    greet(section=next_sec)
    for k in range(1, 4):
        greet(copy=lax.rem(c + k, 4))

    @pl.loop(1, nz)
    def _(k):
        greet(expert=lax.rem(z + k, nz))

    pl.semaphore_wait(barrier, nz - 1 + 3 + 2)

    pend_copy = remote(pend, inc, pend_sem.at[0], pend_sem.at[1], section=prev_sec)
    pend_copy.start()

    logit = log_t[...]
    expd = jnp.exp(logit - jnp.max(logit, axis=0, keepdims=True))
    prob = expd / jnp.sum(expd, axis=0, keepdims=True)
    rid = route_t[...]
    onehot = (iota((EXPERTS, tok), 0) == rid).astype(F32)
    gate = jnp.sum(prob * onehot, axis=0, keepdims=True)
    hot8 = (iota((8, tok), 0) == rid).astype(F32)
    upper = (iota((tok, tok), 0) <= iota((tok, tok), 1)).astype(F32)
    running = mm(hot8.astype(BF16), upper.astype(BF16))
    rank = jnp.sum(running * hot8, axis=0, keepdims=True).astype(I32) - 1
    slot = rid * cp + rank
    placing = (iota((EXPERTS * cp, tok), 0) == slot).astype(F32).astype(BF16)
    gate8 = jnp.broadcast_to(gate, (8, tok)).astype(BF16)
    by_rank = []
    for x in range(EXPERTS):
        rank_x = jnp.where(rid == x, rank, -1)
        by_rank.append((iota((LANES, tok), 0) == rank_x).astype(F32))

    packed = mm(placing, hid[...])
    for x in range(EXPERTS):
        for h in range(2):
            hsend[h, x] = packed[x * cp:(x + 1) * cp, h * half:(h + 1) * half].astype(BF16)

    def first_copy(d):
        other = lax.rem(e + d, EXPERTS)
        return remote(hsend.at[a, other], hbuf.at[a, b, m, e % 2], ha_s.at[d], ha_r.at[e % 2],
                      expert=other * grp + m)

    own_hidden = pltpu.make_async_copy(hsend.at[a, e], hbuf.at[a, b, m, e % 2], own_sem.at[0])

    @pl.when(b == e // 2)
    def _():
        for d in range(1, EXPERTS):
            first_copy(d).start()
        own_hidden.start()

    gate_rows = [
        mm(gate8, by_rank[x].astype(BF16), ((1,), (1,)))[0:1] for x in range(EXPERTS)
    ]

    pend_copy.wait_recv()
    rows = mm(placing, inc[...])
    rid_rows = iota((cp, LANES), 0)
    for x in range(EXPERTS):
        for j in range(grp):
            piece = rows[x * cp:(x + 1) * cp, j * LANES:(j + 1) * LANES]
            rsend[x * grp + j] = jnp.where(rid_rows >= gate_row, gate_rows[x], piece).astype(BF16)

    def row_copy(k):
        dest = lax.rem(z + k, nz)
        return remote(rsend.at[dest], rbuf.at[here], rs.at[k], rr.at[here], expert=dest)

    def row_arrival(k):
        src = lax.rem(z + k, nz)
        return remote(rsend.at[src], rbuf.at[place(src)], rs.at[k], rr.at[place(src)], expert=src)

    def row_pair(i):
        k = nz // 2 - i
        row_copy(k).start()

        @pl.when(k < nz // 2)
        def _():
            row_copy(nz - k).start()

    per_step = nz // 2 // grp

    @pl.loop(0, per_step)
    def _(i):
        row_pair(i)

    own_rows = pltpu.make_async_copy(rsend.at[z], rbuf.at[here], own_sem.at[1])
    own_rows.start()

    def chain_copy(block, way):
        return remote(hbuf.at[a, b, block], hbuf.at[a, b, block], zs.at[way, block], zr.at[block],
                      expert=lax.rem(z + (1 if way == 0 else nz - 1), nz))

    def x_copy(block, h):
        return remote(hbuf.at[h, b, block], hbuf.at[h, b, block], xs.at[block], xr.at[block],
                      copy=(1 - a) * 2 + b)

    def core_copy(block, h, kind, core):
        return remote(hbuf.at[h, core, block], hbuf.at[h, core, block], cs.at[kind, block],
                      cr.at[kind, block], copy=a * 2 + 1 - b)

    for i in range(2):
        @pl.when(2 * b + i != e)
        def _():
            remote(hsend.at[a, 0], hbuf.at[a, b, m, i], ha_s.at[0], ha_r.at[i], expert=m).wait_recv()

    @pl.when(b == e // 2)
    def _():
        own_hidden.wait()

    def spread(block):
        x_copy(block, a).start()
        core_copy(block, a, 0, b).start()

    @pl.when(m < grp - 1)
    def _():
        chain_copy(m, 0).start()

    @pl.when(m > 0)
    def _():
        chain_copy(m, 1).start()

    spread(m)

    @pl.loop(1, grp)
    def _(k):
        @pl.when(m - k >= 0)
        def _():
            chain_copy(m - k, 0).wait_recv()

            @pl.when(m < grp - 1)
            def _():
                chain_copy(m - k, 0).start()

            spread(m - k)

        @pl.when(m + k < grp)
        def _():
            chain_copy(m + k, 1).wait_recv()

            @pl.when(m > 0)
            def _():
                chain_copy(m + k, 1).start()

            spread(m + k)

        for i in range(per_step):
            row_pair(k * per_step + i)

    @pl.loop(0, grp)
    def _(block):
        x_copy(block, 1 - a).wait_recv()
        core_copy(block, 1 - a, 1, b).start()

    n_blocks = plan.shape[1]
    most = psend.shape[1] // PUSH_ROWS
    owner = plan[...]
    owner_hot = (iota((nz, n_blocks), 0) == owner).astype(F32)
    before = (iota((n_blocks, n_blocks), 0) < iota((n_blocks, n_blocks), 1)).astype(F32)
    earlier = mm(owner_hot.astype(BF16), before.astype(BF16))
    block_rank = jnp.sum(earlier * owner_hot, axis=0, keepdims=True)
    block_slot = jnp.broadcast_to(owner.astype(F32) * most + block_rank, (8, n_blocks))
    widen = (iota((n_blocks, ff), 1) // PUSH_ROWS == iota((n_blocks, ff), 0)).astype(F32)
    key = mm(block_slot.astype(BF16), widen.astype(BF16))[0:1].astype(I32)
    key = key * PUSH_ROWS + iota((1, ff), 1) % PUSH_ROWS
    big[...] = (iota((nz * most * PUSH_ROWS, ff), 0) == key).astype(F32).astype(BF16)

    for load in loads:
        load.wait()

    @pl.loop(0, grp)
    def _(block):
        core_copy(block, a, 0, 1 - b).wait_recv()
        core_copy(block, 1 - a, 1, 1 - b).wait_recv()

    own_rows.wait()

    @pl.loop(1, nz)
    def _(k):
        row_arrival(k).wait_recv()

    def flat(blocks):
        return blocks.astype(F32).reshape(nz * cp, blocks.shape[-1])

    gates[...] = jnp.zeros(gates.shape, F32)
    for p in range(nz):
        gates[p:p + 1, :] = rbuf[p].astype(F32)[gate_row:gate_row + 1]
    gate_cols = gates[...].T
    for p in range(nz):
        scaled[p] = gate_cols[0:cp, p:p + 1] * rbuf[p].astype(F32)
    scaled_all = scaled[...].reshape(nz * cp, LANES).astype(BF16)
    for h in range(2):
        hidden_h = flat(hbuf[h]).astype(BF16)
        hflat[h] = hidden_h
        grad = mm(scaled_all, hidden_h, ((0,), (0,))).T
        rows_h = pl.ds(h * half, half)
        first = beta_first * m1v[rows_h, :] + (1.0 - beta_first) * grad
        second = beta_second * m2v[rows_h, :] + (1.0 - beta_second) * grad * grad
        update = first / bias_first / (jnp.sqrt(second / bias_second) + adam_eps) + decay_rate * mav[rows_h, :]
        new = mav[rows_h, :] - learn_rate * update
        m1v[rows_h, :] = first
        m2v[rows_h, :] = second
        mav[rows_h, :] = new
        fresh[rows_h, :] = new.astype(BF16)
    outputs = mm(hflat[0], wv[0:half, :]) + mm(hflat[1], wv[half:ff, :])
    product = outputs * flat(rbuf[...])
    shares = mm(jnp.ones((8, LANES), F32), product, ((1,), (1,)), HIGHEST)
    for p in range(nz):
        ret_s[p, :, 0:cp] = shares[0:1, p * cp:(p + 1) * cp]

    def ret_copy(k):
        dest = lax.rem(z + k, nz)
        return remote(ret_s.at[place(dest)], ret_r.at[z], gs.at[k], gr.at[z], expert=dest)

    def ret_arrival(k):
        src = lax.rem(z + k, nz)
        return remote(ret_s.at[src], ret_r.at[src], gs.at[k], gr.at[src], expert=src)

    @pl.loop(0, nz // 2)
    def _(i):
        k = nz // 2 - i
        ret_copy(k).start()

        @pl.when(k < nz // 2)
        def _():
            ret_copy(nz - k).start()

    per_owner = most * PUSH_ROWS
    for x in range(EXPERTS):
        part = mm(big[x * grp * per_owner:(x + 1) * grp * per_owner, :], fresh[...])
        for j in range(grp):
            psend[x * grp + j] = part[j * per_owner:(j + 1) * per_owner].astype(BF16)

    def push_copy(k):
        dest = lax.rem(z + k, nz)
        return remote(psend.at[dest], serv.at[z], ps.at[k], pr.at[z], expert=dest)

    def push_arrival(k):
        src = lax.rem(z + k, nz)
        return remote(psend.at[src], serv.at[src], ps.at[k], pr.at[src], expert=src)

    @pl.loop(0, nz // 2)
    def _(i):
        k = nz // 2 - i
        push_copy(k).start()

        @pl.when(k < nz // 2)
        def _():
            push_copy(nz - k).start()

    own_push = pltpu.make_async_copy(psend.at[z], serv.at[z], own_sem.at[2])
    own_push.start()
    stores = [
        pltpu.make_async_copy(src, dst, st_sem.at[i])
        for i, (src, dst) in enumerate(((m1v, m1_out), (m2v, m2_out), (mav, ma_out)))
    ]
    for store in stores:
        store.start()

    own_ret = pltpu.make_async_copy(ret_s.at[here], ret_r.at[z], own_sem.at[3])
    own_ret.start()
    own_ret.wait()

    @pl.loop(1, nz)
    def _(k):
        ret_arrival(k).wait_recv()

    for x in range(EXPERTS):
        total = ret_r[x * grp]
        for j in range(1, grp):
            total = total + ret_r[x * grp + j]
        cp_s[x:x + 1, :] = total

    def share_copy(k):
        return remote(cp_s, cp_r.at[k], ks.at[k], kr.at[k], copy=lax.rem(c + k, 4))

    for k in range(1, 4):
        share_copy(k).start()
    for k in range(1, 4):
        share_copy(k).wait_recv()
    whole = cp_s[...] + cp_r[1] + cp_r[2] + cp_r[3]
    whole = jnp.where(iota(whole.shape, 1) < cp, whole, 0.0)
    gate_grad = jnp.zeros((8, tok), F32)
    for x in range(EXPERTS):
        gate_grad += mm(jnp.broadcast_to(whole[x:x + 1], (8, LANES)), by_rank[x], precision=HIGHEST)
    logit_grad = (gate_grad[0:1] * gate) * (onehot - prob)
    gates[0:EXPERTS, :] = logit_grad
    grad_cols = gates[...].T
    term = inc[...].astype(F32)
    extra = grad_cols[:, 0:1] * rw_t[0:1, :]
    for x in range(1, EXPERTS):
        extra += grad_cols[:, x:x + 1] * rw_t[x:x + 1, :]
    ig_out[...] = (term + extra).astype(BF16)

    pend_copy.wait_send()
    for k in range(1, 4):
        share_copy(k).wait_send()

    @pl.when(b == e // 2)
    def _():
        for d in range(1, EXPERTS):
            first_copy(d).wait_send()

    @pl.loop(0, grp)
    def _(block):
        @pl.when((block <= m) & (m < grp - 1))
        def _():
            chain_copy(block, 0).wait_send()

        @pl.when((block >= m) & (m > 0))
        def _():
            chain_copy(block, 1).wait_send()

        x_copy(block, a).wait_send()
        core_copy(block, a, 0, b).wait_send()
        core_copy(block, 1 - a, 1, b).wait_send()

    @pl.loop(1, nz)
    def _(k):
        row_copy(k).wait_send()
        ret_copy(k).wait_send()

    for store in stores:
        store.wait()
    own_push.wait()

    @pl.loop(1, nz)
    def _(k):
        push_copy(k).wait_send()
        push_arrival(k).wait_recv()


def per_device(
    pending, hidden, logits, routes, router_weight, down_weight, master, moment_first, moment_second, push_plan,
):
    n_sec, nz = lax.axis_size("section"), lax.axis_size("expert")
    tok, width = pending.shape[1:]
    ff = hidden.shape[2]
    grp = nz // EXPERTS
    capacity = tok * 9 // (EXPERTS * 8)
    cp = 40
    gate_row = 36
    n_blocks = ff // PUSH_ROWS
    most = max(2, (3 * n_blocks + 2 * nz - 1) // (2 * nz))
    assert capacity <= gate_row and width == grp * LANES and tok == LANES
    per_owner = most * PUSH_ROWS
    half = ff // 2
    vmem, hbm = pl.BlockSpec(memory_space=pltpu.VMEM), pl.BlockSpec(memory_space=pl.ANY)
    dma = pltpu.SemaphoreType.DMA
    piece = jax.ShapeDtypeStruct((ff, LANES), F32)
    input_grad, fresh_master, first, second, serving = pl.pallas_call(
        functools.partial(kernel, n_sec, nz, cp, gate_row),
        out_shape=(
            jax.ShapeDtypeStruct((tok, width), BF16), piece, piece, piece,
            jax.ShapeDtypeStruct((nz, per_owner, LANES), BF16),
        ),
        in_specs=[hbm] + [vmem] * 4 + [hbm] * 4 + [vmem],
        out_specs=[vmem] + [hbm] * 4,
        scratch_shapes=[
            pltpu.VMEM((tok, width), BF16),
            pltpu.VMEM((2, EXPERTS, cp, half), BF16),
            pltpu.VMEM((2, 2, grp, 2, cp, half), BF16),
            pltpu.VMEM((2, nz * cp, half), BF16),
            pltpu.VMEM((nz, cp, LANES), BF16),
            pltpu.VMEM((nz, cp, LANES), BF16),
            pltpu.VMEM((nz, cp, LANES), F32),
            pltpu.VMEM((LANES, LANES), F32),
            pltpu.VMEM((nz * per_owner, ff), BF16),
            pltpu.VMEM((nz, per_owner, LANES), BF16),
            pltpu.VMEM((nz, 1, LANES), F32),
            pltpu.VMEM((nz, 1, LANES), F32),
            pltpu.VMEM((EXPERTS, LANES), F32),
            pltpu.VMEM((4, EXPERTS, LANES), F32),
            pltpu.VMEM((ff, LANES), BF16),
            pltpu.VMEM((ff, LANES), F32),
            pltpu.VMEM((ff, LANES), F32),
            pltpu.VMEM((ff, LANES), F32),
            pltpu.VMEM((ff, LANES), BF16),
            dma((4,)), dma((3,)), dma((2,)), dma((4,)),
            dma((EXPERTS,)), dma((2,)),
            dma((2, grp)), dma((grp,)),
            dma((grp,)), dma((grp,)),
            dma((2, grp)), dma((2, grp)),
            dma((nz,)), dma((nz,)),
            dma((nz,)), dma((nz,)),
            dma((nz,)), dma((nz,)),
            dma((4,)), dma((4,)),
        ],
        compiler_params=pltpu.CompilerParams(
            collective_id=0, has_side_effects=True, vmem_limit_bytes=63 * 1024 * 1024
        ),
        cost_estimate=pl.CostEstimate(flops=10**9, bytes_accessed=8 * 10**6, transcendentals=10**5),
    )(
        pending[0], hidden[0], logits[0].T, routes[0].T, router_weight[0].T,
        down_weight[0, 0], master[0, 0], moment_first[0, 0], moment_second[0, 0], push_plan[0, 0, 0].T,
    )
    return (
        input_grad[None],
        fresh_master[None, None],
        first[None, None],
        second[None, None],
        serving.reshape(nz * most, PUSH_ROWS, LANES)[None, None, None],
    )


def solution(mesh):
    return jax.shard_map(
        per_device,
        mesh=mesh,
        in_specs=(
            P("section", "expert", "copy"),
            P("section", "expert", None),
            P("section", "expert", None),
            P("section", "expert", None),
            P("section", "copy", None),
            P("section", "copy", None, "expert"),
            P("section", "copy", None, "expert"),
            P("section", "copy", None, "expert"),
            P("section", "copy", None, "expert"),
            P("section", "copy", "expert", None, None),
        ),
        out_specs=(
            P("section", "expert", "copy"),
            P("section", "copy", None, "expert"),
            P("section", "copy", None, "expert"),
            P("section", "copy", None, "expert"),
            P("section", "copy", "expert", None, None, None),
        ),
        check_vma=False,
    )
```

```python
import functools

import jax
import jax.numpy as jnp
from jax import lax
from jax.experimental import pallas as pl
from jax.experimental.pallas import tpu as pltpu
from jax.sharding import PartitionSpec as P

PUSH_ROWS = 8
EXPERTS = 4
LANES = 128

beta_first = 0.9
beta_second = 0.95
learn_rate = 0.002
decay_rate = 0.1
adam_eps = 1e-08
bias_first = 1.0 - 0.9**10
bias_second = 1.0 - 0.95**10

F32 = jnp.float32
BF16 = jnp.bfloat16
I32 = jnp.int32
HIGHEST = lax.Precision.HIGHEST


def iota(shape, dim):
    return lax.broadcasted_iota(I32, shape, dim)


def mm(x, y, dims=((1,), (0,)), precision=None):
    return lax.dot_general(x, y, (dims, ((), ())), precision=precision, preferred_element_type=F32)


def kernel(
    n_sec, nz, slot_rows, gate_row,
    pend, hid, log_t, route_t, rw_t, w_hbm, ma_hbm, m1_hbm, m2_hbm, plan,
    ig_out, ma_out, m1_out, m2_out, serv,
    inc, hsend, hbuf, hflat, rsend, rbuf, scaled, gates, big, psend, ret_s, ret_r, cp_s, cp_r,
    wv, mav, m1v, m2v, fresh,
    ld_sem, st_sem, pend_sem, own_sem, ha_s, ha_r, zs, zr, xs, xr, cs, cr, rs, rr, ps, pr, gs, gr, ks, kr,
):
    grp = nz // EXPERTS
    cp = slot_rows
    tok = hid.shape[0]
    half = hid.shape[1] // 2
    ff = 2 * half
    s, z, c = lax.axis_index("section"), lax.axis_index("expert"), lax.axis_index("copy")
    a, b = c // 2, c % 2
    e, m = z // grp, z % grp
    here = (e // 2) * (2 * grp) + m * 2 + e % 2

    def place(p):
        q = p // grp
        return (q // 2) * (2 * grp) + (p % grp) * 2 + q % 2

    def remote(src, dst, send, recv, **axis):
        return pltpu.make_async_remote_copy(
            src_ref=src, dst_ref=dst, send_sem=send, recv_sem=recv,
            device_id=axis, device_id_type=pl.DeviceIdType.MESH,
        )

    loads = [
        pltpu.make_async_copy(src, dst, ld_sem.at[i])
        for i, (src, dst) in enumerate(((w_hbm, wv), (m1_hbm, m1v), (m2_hbm, m2v), (ma_hbm, mav)))
    ]
    for load in loads:
        load.start()

    barrier = pltpu.get_barrier_semaphore()
    prev_sec, next_sec = lax.rem(s + n_sec - 1, n_sec), lax.rem(s + 1, n_sec)

    def greet(**axis):
        pl.semaphore_signal(barrier, inc=1, device_id=axis, device_id_type=pl.DeviceIdType.MESH)

    greet(section=prev_sec)
    greet(section=next_sec)
    for k in range(1, 4):
        greet(copy=lax.rem(c + k, 4))

    @pl.loop(1, nz)
    def _(k):
        greet(expert=lax.rem(z + k, nz))

    pl.semaphore_wait(barrier, nz - 1 + 3 + 2)

    pend_copy = remote(pend, inc, pend_sem.at[0], pend_sem.at[1], section=prev_sec)
    pend_copy.start()

    logit = log_t[...]
    expd = jnp.exp(logit - jnp.max(logit, axis=0, keepdims=True))
    prob = expd / jnp.sum(expd, axis=0, keepdims=True)
    rid = route_t[...]
    onehot = (iota((EXPERTS, tok), 0) == rid).astype(F32)
    gate = jnp.sum(prob * onehot, axis=0, keepdims=True)
    hot8 = (iota((8, tok), 0) == rid).astype(F32)
    upper = (iota((tok, tok), 0) <= iota((tok, tok), 1)).astype(F32)
    running = mm(hot8.astype(BF16), upper.astype(BF16))
    rank = jnp.sum(running * hot8, axis=0, keepdims=True).astype(I32) - 1
    slot = rid * cp + rank
    placing = (iota((EXPERTS * cp, tok), 0) == slot).astype(F32).astype(BF16)
    gate8 = jnp.broadcast_to(gate, (8, tok)).astype(BF16)
    by_rank = []
    for x in range(EXPERTS):
        rank_x = jnp.where(rid == x, rank, -1)
        by_rank.append((iota((LANES, tok), 0) == rank_x).astype(F32))

    packed = mm(placing, hid[...])
    for x in range(EXPERTS):
        for h in range(2):
            hsend[h, x] = packed[x * cp:(x + 1) * cp, h * half:(h + 1) * half].astype(BF16)

    def first_copy(d):
        other = lax.rem(e + d, EXPERTS)
        return remote(hsend.at[a, other], hbuf.at[a, b, m, e % 2], ha_s.at[d], ha_r.at[e % 2],
                      expert=other * grp + m)

    own_hidden = pltpu.make_async_copy(hsend.at[a, e], hbuf.at[a, b, m, e % 2], own_sem.at[0])

    @pl.when(b == e // 2)
    def _():
        for d in range(1, EXPERTS):
            first_copy(d).start()
        own_hidden.start()

    gate_rows = [
        mm(gate8, by_rank[x].astype(BF16), ((1,), (1,)))[0:1] for x in range(EXPERTS)
    ]

    pend_copy.wait_recv()
    rows = mm(placing, inc[...])
    rid_rows = iota((cp, LANES), 0)
    for x in range(EXPERTS):
        for j in range(grp):
            piece = rows[x * cp:(x + 1) * cp, j * LANES:(j + 1) * LANES]
            rsend[x * grp + j] = jnp.where(rid_rows >= gate_row, gate_rows[x], piece).astype(BF16)

    def row_copy(k):
        dest = lax.rem(z + k, nz)
        return remote(rsend.at[dest], rbuf.at[here], rs.at[k], rr.at[here], expert=dest)

    def row_arrival(k):
        src = lax.rem(z + k, nz)
        return remote(rsend.at[src], rbuf.at[place(src)], rs.at[k], rr.at[place(src)], expert=src)

    def row_pair(i):
        k = nz // 2 - i
        row_copy(k).start()

        @pl.when(k < nz // 2)
        def _():
            row_copy(nz - k).start()

    per_step = nz // 2 // grp

    @pl.loop(0, per_step)
    def _(i):
        row_pair(i)

    own_rows = pltpu.make_async_copy(rsend.at[z], rbuf.at[here], own_sem.at[1])
    own_rows.start()

    def chain_copy(block, way):
        return remote(hbuf.at[a, b, block], hbuf.at[a, b, block], zs.at[way, block], zr.at[block],
                      expert=lax.rem(z + (1 if way == 0 else nz - 1), nz))

    def x_copy(block, h):
        return remote(hbuf.at[h, b, block], hbuf.at[h, b, block], xs.at[block], xr.at[block],
                      copy=(1 - a) * 2 + b)

    def core_copy(block, h, kind, core):
        return remote(hbuf.at[h, core, block], hbuf.at[h, core, block], cs.at[kind, block],
                      cr.at[kind, block], copy=a * 2 + 1 - b)

    for i in range(2):
        @pl.when(2 * b + i != e)
        def _():
            remote(hsend.at[a, 0], hbuf.at[a, b, m, i], ha_s.at[0], ha_r.at[i], expert=m).wait_recv()

    @pl.when(b == e // 2)
    def _():
        own_hidden.wait()

    def spread(block):
        x_copy(block, a).start()
        core_copy(block, a, 0, b).start()

    @pl.when(m < grp - 1)
    def _():
        chain_copy(m, 0).start()

    @pl.when(m > 0)
    def _():
        chain_copy(m, 1).start()

    spread(m)

    @pl.loop(1, grp)
    def _(k):
        @pl.when(m - k >= 0)
        def _():
            chain_copy(m - k, 0).wait_recv()

            @pl.when(m < grp - 1)
            def _():
                chain_copy(m - k, 0).start()

            spread(m - k)

        @pl.when(m + k < grp)
        def _():
            chain_copy(m + k, 1).wait_recv()

            @pl.when(m > 0)
            def _():
                chain_copy(m + k, 1).start()

            spread(m + k)

        for i in range(per_step):
            row_pair(k * per_step + i)

    @pl.loop(0, grp)
    def _(block):
        x_copy(block, 1 - a).wait_recv()
        core_copy(block, 1 - a, 1, b).start()

    n_blocks = plan.shape[1]
    most = psend.shape[1] // PUSH_ROWS
    owner = plan[...]
    owner_hot = (iota((nz, n_blocks), 0) == owner).astype(F32)
    before = (iota((n_blocks, n_blocks), 0) < iota((n_blocks, n_blocks), 1)).astype(F32)
    earlier = mm(owner_hot.astype(BF16), before.astype(BF16))
    block_rank = jnp.sum(earlier * owner_hot, axis=0, keepdims=True)
    block_slot = jnp.broadcast_to(owner.astype(F32) * most + block_rank, (8, n_blocks))
    widen = (iota((n_blocks, ff), 1) // PUSH_ROWS == iota((n_blocks, ff), 0)).astype(F32)
    key = mm(block_slot.astype(BF16), widen.astype(BF16))[0:1].astype(I32)
    key = key * PUSH_ROWS + iota((1, ff), 1) % PUSH_ROWS
    big[...] = (iota((nz * most * PUSH_ROWS, ff), 0) == key).astype(F32).astype(BF16)

    for load in loads:
        load.wait()

    @pl.loop(0, grp)
    def _(block):
        core_copy(block, a, 0, 1 - b).wait_recv()
        core_copy(block, 1 - a, 1, 1 - b).wait_recv()

    own_rows.wait()

    @pl.loop(1, nz)
    def _(k):
        row_arrival(k).wait_recv()

    def flat(blocks):
        return blocks.astype(F32).reshape(nz * cp, blocks.shape[-1])

    gates[...] = jnp.zeros(gates.shape, F32)
    for p in range(nz):
        gates[p:p + 1, :] = rbuf[p].astype(F32)[gate_row:gate_row + 1]
    gate_cols = gates[...].T
    for p in range(nz):
        scaled[p] = gate_cols[0:cp, p:p + 1] * rbuf[p].astype(F32)
    scaled_all = scaled[...].reshape(nz * cp, LANES).astype(BF16)
    for h in range(2):
        hidden_h = flat(hbuf[h]).astype(BF16)
        hflat[h] = hidden_h
        grad = mm(scaled_all, hidden_h, ((0,), (0,))).T
        rows_h = pl.ds(h * half, half)
        first = beta_first * m1v[rows_h, :] + (1.0 - beta_first) * grad
        second = beta_second * m2v[rows_h, :] + (1.0 - beta_second) * grad * grad
        update = first / bias_first / (jnp.sqrt(second / bias_second) + adam_eps) + decay_rate * mav[rows_h, :]
        new = mav[rows_h, :] - learn_rate * update
        m1v[rows_h, :] = first
        m2v[rows_h, :] = second
        mav[rows_h, :] = new
        fresh[rows_h, :] = new.astype(BF16)
    per_owner = most * PUSH_ROWS
    for x in range(EXPERTS):
        part = mm(big[x * grp * per_owner:(x + 1) * grp * per_owner, :], fresh[...])
        for j in range(grp):
            psend[x * grp + j] = part[j * per_owner:(j + 1) * per_owner].astype(BF16)

    def push_copy(k):
        dest = lax.rem(z + k, nz)
        return remote(psend.at[dest], serv.at[z], ps.at[k], pr.at[z], expert=dest)

    def push_arrival(k):
        src = lax.rem(z + k, nz)
        return remote(psend.at[src], serv.at[src], ps.at[k], pr.at[src], expert=src)

    def push_pair(i):
        k = nz // 2 - i
        push_copy(k).start()

        @pl.when(k < nz // 2)
        def _():
            push_copy(nz - k).start()

    early = nz // 8

    @pl.loop(0, early)
    def _(i):
        push_pair(i)

    outputs = mm(hflat[0], wv[0:half, :]) + mm(hflat[1], wv[half:ff, :])
    product = outputs * flat(rbuf[...])
    shares = mm(jnp.ones((8, LANES), F32), product, ((1,), (1,)), HIGHEST)
    for p in range(nz):
        ret_s[p, :, 0:cp] = shares[0:1, p * cp:(p + 1) * cp]

    def ret_copy(k):
        dest = lax.rem(z + k, nz)
        return remote(ret_s.at[place(dest)], ret_r.at[z], gs.at[k], gr.at[z], expert=dest)

    def ret_arrival(k):
        src = lax.rem(z + k, nz)
        return remote(ret_s.at[src], ret_r.at[src], gs.at[k], gr.at[src], expert=src)

    @pl.loop(0, nz // 2)
    def _(i):
        k = nz // 2 - i
        ret_copy(k).start()

        @pl.when(k < nz // 2)
        def _():
            ret_copy(nz - k).start()

    @pl.loop(early, nz // 2)
    def _(i):
        push_pair(i)

    own_push = pltpu.make_async_copy(psend.at[z], serv.at[z], own_sem.at[2])
    own_push.start()
    stores = [
        pltpu.make_async_copy(src, dst, st_sem.at[i])
        for i, (src, dst) in enumerate(((m1v, m1_out), (m2v, m2_out), (mav, ma_out)))
    ]
    for store in stores:
        store.start()

    own_ret = pltpu.make_async_copy(ret_s.at[here], ret_r.at[z], own_sem.at[3])
    own_ret.start()
    own_ret.wait()

    @pl.loop(1, nz)
    def _(k):
        ret_arrival(k).wait_recv()

    for x in range(EXPERTS):
        total = ret_r[x * grp]
        for j in range(1, grp):
            total = total + ret_r[x * grp + j]
        cp_s[x:x + 1, :] = total

    def share_copy(k):
        return remote(cp_s, cp_r.at[k], ks.at[k], kr.at[k], copy=lax.rem(c + k, 4))

    for k in range(1, 4):
        share_copy(k).start()
    for k in range(1, 4):
        share_copy(k).wait_recv()
    whole = cp_s[...] + cp_r[1] + cp_r[2] + cp_r[3]
    whole = jnp.where(iota(whole.shape, 1) < cp, whole, 0.0)
    gate_grad = jnp.zeros((8, tok), F32)
    for x in range(EXPERTS):
        gate_grad += mm(jnp.broadcast_to(whole[x:x + 1], (8, LANES)), by_rank[x], precision=HIGHEST)
    logit_grad = (gate_grad[0:1] * gate) * (onehot - prob)
    gates[0:EXPERTS, :] = logit_grad
    grad_cols = gates[...].T
    term = inc[...].astype(F32)
    extra = grad_cols[:, 0:1] * rw_t[0:1, :]
    for x in range(1, EXPERTS):
        extra += grad_cols[:, x:x + 1] * rw_t[x:x + 1, :]
    inc[...] = (term + extra).astype(BF16)
    stores.append(pltpu.make_async_copy(inc, ig_out, st_sem.at[3]))
    stores[3].start()

    pend_copy.wait_send()
    for k in range(1, 4):
        share_copy(k).wait_send()

    @pl.when(b == e // 2)
    def _():
        for d in range(1, EXPERTS):
            first_copy(d).wait_send()

    @pl.loop(0, grp)
    def _(block):
        @pl.when((block <= m) & (m < grp - 1))
        def _():
            chain_copy(block, 0).wait_send()

        @pl.when((block >= m) & (m > 0))
        def _():
            chain_copy(block, 1).wait_send()

        x_copy(block, a).wait_send()
        core_copy(block, a, 0, b).wait_send()
        core_copy(block, 1 - a, 1, b).wait_send()

    @pl.loop(1, nz)
    def _(k):
        row_copy(k).wait_send()
        ret_copy(k).wait_send()

    for store in stores:
        store.wait()
    own_push.wait()

    @pl.loop(1, nz)
    def _(k):
        push_copy(k).wait_send()
        push_arrival(k).wait_recv()


def hand_over(n, *refs):
    sources, dests, held, sems = refs[:n], refs[n:2 * n], refs[2 * n:3 * n], refs[3 * n]
    fetches = [pltpu.make_async_copy(sources[i], held[i], sems.at[0, i]) for i in range(n)]
    stores = [pltpu.make_async_copy(held[i], dests[i], sems.at[1, i]) for i in range(n)]
    for fetch in fetches:
        fetch.start()
    for fetch, store in zip(fetches, stores):
        fetch.wait()
        store.start()
    for store in stores:
        store.wait()


def per_device(
    pending, hidden, logits, routes, router_weight, down_weight, master, moment_first, moment_second, push_plan,
):
    n_sec, nz = lax.axis_size("section"), lax.axis_size("expert")
    tok, width = pending.shape[1:]
    ff = hidden.shape[2]
    grp = nz // EXPERTS
    capacity = tok * 9 // (EXPERTS * 8)
    cp = 40
    gate_row = 36
    n_blocks = ff // PUSH_ROWS
    most = max(2, (3 * n_blocks + 2 * nz - 1) // (2 * nz))
    assert capacity <= gate_row and width == grp * LANES and tok == LANES
    per_owner = most * PUSH_ROWS
    half = ff // 2
    vmem, hbm = pl.BlockSpec(memory_space=pltpu.VMEM), pl.BlockSpec(memory_space=pl.ANY)
    dma = pltpu.SemaphoreType.DMA
    piece = jax.ShapeDtypeStruct((ff, LANES), F32)
    results = pl.pallas_call(
        functools.partial(kernel, n_sec, nz, cp, gate_row),
        out_shape=(
            jax.ShapeDtypeStruct((tok, width), BF16), piece, piece, piece,
            jax.ShapeDtypeStruct((nz, per_owner, LANES), BF16),
        ),
        in_specs=[hbm] + [vmem] * 4 + [hbm] * 4 + [vmem],
        out_specs=[hbm] * 5,
        scratch_shapes=[
            pltpu.VMEM((tok, width), BF16),
            pltpu.VMEM((2, EXPERTS, cp, half), BF16),
            pltpu.VMEM((2, 2, grp, 2, cp, half), BF16),
            pltpu.VMEM((2, nz * cp, half), BF16),
            pltpu.VMEM((nz, cp, LANES), BF16),
            pltpu.VMEM((nz, cp, LANES), BF16),
            pltpu.VMEM((nz, cp, LANES), F32),
            pltpu.VMEM((LANES, LANES), F32),
            pltpu.VMEM((nz * per_owner, ff), BF16),
            pltpu.VMEM((nz, per_owner, LANES), BF16),
            pltpu.VMEM((nz, 1, LANES), F32),
            pltpu.VMEM((nz, 1, LANES), F32),
            pltpu.VMEM((EXPERTS, LANES), F32),
            pltpu.VMEM((4, EXPERTS, LANES), F32),
            pltpu.VMEM((ff, LANES), BF16),
            pltpu.VMEM((ff, LANES), F32),
            pltpu.VMEM((ff, LANES), F32),
            pltpu.VMEM((ff, LANES), F32),
            pltpu.VMEM((ff, LANES), BF16),
            dma((4,)), dma((4,)), dma((2,)), dma((4,)),
            dma((EXPERTS,)), dma((2,)),
            dma((2, grp)), dma((grp,)),
            dma((grp,)), dma((grp,)),
            dma((2, grp)), dma((2, grp)),
            dma((nz,)), dma((nz,)),
            dma((nz,)), dma((nz,)),
            dma((nz,)), dma((nz,)),
            dma((4,)), dma((4,)),
        ],
        compiler_params=pltpu.CompilerParams(
            collective_id=0, has_side_effects=True, vmem_limit_bytes=63 * 1024 * 1024
        ),
        cost_estimate=pl.CostEstimate(flops=10**9, bytes_accessed=8 * 10**6, transcendentals=10**5),
    )(
        pending[0], hidden[0], logits[0].T, routes[0].T, router_weight[0].T,
        down_weight[0, 0], master[0, 0], moment_first[0, 0], moment_second[0, 0], push_plan[0, 0, 0].T,
    )
    n = len(results)
    input_grad, fresh_master, first, second, serving = pl.pallas_call(
        functools.partial(hand_over, n),
        out_shape=tuple(jax.ShapeDtypeStruct(r.shape, r.dtype) for r in results),
        in_specs=[hbm] * n,
        out_specs=[hbm] * n,
        scratch_shapes=[pltpu.VMEM(r.shape, r.dtype) for r in results] + [dma((2, n))],
        compiler_params=pltpu.CompilerParams(vmem_limit_bytes=63 * 1024 * 1024),
        cost_estimate=pl.CostEstimate(flops=0, bytes_accessed=4 * 10**6, transcendentals=0),
    )(*results)
    return (
        input_grad[None],
        fresh_master[None, None],
        first[None, None],
        second[None, None],
        serving.reshape(nz * most, PUSH_ROWS, LANES)[None, None, None],
    )


def solution(mesh):
    return jax.shard_map(
        per_device,
        mesh=mesh,
        in_specs=(
            P("section", "expert", "copy"),
            P("section", "expert", None),
            P("section", "expert", None),
            P("section", "expert", None),
            P("section", "copy", None),
            P("section", "copy", None, "expert"),
            P("section", "copy", None, "expert"),
            P("section", "copy", None, "expert"),
            P("section", "copy", None, "expert"),
            P("section", "copy", "expert", None, None),
        ),
        out_specs=(
            P("section", "expert", "copy"),
            P("section", "copy", None, "expert"),
            P("section", "copy", None, "expert"),
            P("section", "copy", None, "expert"),
            P("section", "copy", "expert", None, None, None),
        ),
        check_vma=False,
    )
```

```python
import functools

import jax
import jax.numpy as jnp
from jax import lax
from jax.experimental import pallas as pl
from jax.experimental.pallas import tpu as pltpu
from jax.sharding import PartitionSpec as P

PUSH_ROWS = 8
EXPERTS = 4
LANES = 128

beta_first = 0.9
beta_second = 0.95
learn_rate = 0.002
decay_rate = 0.1
adam_eps = 1e-08
bias_first = 1.0 - 0.9**10
bias_second = 1.0 - 0.95**10

F32 = jnp.float32
BF16 = jnp.bfloat16
I32 = jnp.int32
HIGHEST = lax.Precision.HIGHEST


def iota(shape, dim):
    return lax.broadcasted_iota(I32, shape, dim)


def mm(x, y, dims=((1,), (0,)), precision=None):
    return lax.dot_general(x, y, (dims, ((), ())), precision=precision, preferred_element_type=F32)


def kernel(
    n_sec, nz, slot_rows, gate_row,
    pend, hid, log_t, route_t, rw_t, w_hbm, ma_hbm, m1_hbm, m2_hbm, plan,
    ig_out, ma_out, m1_out, m2_out, serv,
    inc, hsend, hbuf, hflat, outs, rsend, rbuf, scaled, gates, big, psend, ret_s, ret_r, cp_s, cp_r,
    wv, mav, m1v, m2v, fresh,
    ld_sem, st_sem, pend_sem, own_sem, ha_s, ha_r, zs, zr, xs, xr, cs, cr, rs, rr, ps, pr, gs, gr, ks, kr,
):
    grp = nz // EXPERTS
    cp = slot_rows
    tok = hid.shape[0]
    half = hid.shape[1] // 2
    ff = 2 * half
    s, z, c = lax.axis_index("section"), lax.axis_index("expert"), lax.axis_index("copy")
    a, b = c // 2, c % 2
    e, m = z // grp, z % grp
    here = (e // 2) * (2 * grp) + m * 2 + e % 2

    def place(p):
        q = p // grp
        return (q // 2) * (2 * grp) + (p % grp) * 2 + q % 2

    def remote(src, dst, send, recv, **axis):
        return pltpu.make_async_remote_copy(
            src_ref=src, dst_ref=dst, send_sem=send, recv_sem=recv,
            device_id=axis, device_id_type=pl.DeviceIdType.MESH,
        )

    loads = [
        pltpu.make_async_copy(src, dst, ld_sem.at[i])
        for i, (src, dst) in enumerate(((w_hbm, wv), (m1_hbm, m1v), (m2_hbm, m2v), (ma_hbm, mav)))
    ]
    for load in loads:
        load.start()

    barrier = pltpu.get_barrier_semaphore()
    prev_sec, next_sec = lax.rem(s + n_sec - 1, n_sec), lax.rem(s + 1, n_sec)

    def greet(**axis):
        pl.semaphore_signal(barrier, inc=1, device_id=axis, device_id_type=pl.DeviceIdType.MESH)

    @pl.loop(0, nz // 2)
    def _(i):
        k = nz // 2 - i
        greet(expert=lax.rem(z + k, nz))

        @pl.when(k < nz // 2)
        def _():
            greet(expert=lax.rem(z + nz - k, nz))

    greet(section=prev_sec)
    greet(section=next_sec)
    for k in range(1, 4):
        greet(copy=lax.rem(c + k, 4))

    logit = log_t[...]
    expd = jnp.exp(logit - jnp.max(logit, axis=0, keepdims=True))
    prob = expd / jnp.sum(expd, axis=0, keepdims=True)
    rid = route_t[...]
    onehot = (iota((EXPERTS, tok), 0) == rid).astype(F32)
    gate = jnp.sum(prob * onehot, axis=0, keepdims=True)
    hot8 = (iota((8, tok), 0) == rid).astype(F32)
    upper = (iota((tok, tok), 0) <= iota((tok, tok), 1)).astype(F32)
    running = mm(hot8.astype(BF16), upper.astype(BF16))
    rank = jnp.sum(running * hot8, axis=0, keepdims=True).astype(I32) - 1
    slot = rid * cp + rank
    placing = (iota((EXPERTS * cp, tok), 0) == slot).astype(F32).astype(BF16)
    gate8 = jnp.broadcast_to(gate, (8, tok)).astype(BF16)
    by_rank = []
    for x in range(EXPERTS):
        rank_x = jnp.where(rid == x, rank, -1)
        by_rank.append((iota((LANES, tok), 0) == rank_x).astype(F32))

    packed = mm(placing, hid[...])
    for x in range(EXPERTS):
        for h in range(2):
            hsend[h, x] = packed[x * cp:(x + 1) * cp, h * half:(h + 1) * half].astype(BF16)

    gate_rows = [
        mm(gate8, by_rank[x].astype(BF16), ((1,), (1,)))[0:1] for x in range(EXPERTS)
    ]

    n_blocks = plan.shape[1]
    most = psend.shape[1] // PUSH_ROWS
    owner = plan[...]
    owner_hot = (iota((nz, n_blocks), 0) == owner).astype(F32)
    before = (iota((n_blocks, n_blocks), 0) < iota((n_blocks, n_blocks), 1)).astype(F32)
    earlier = mm(owner_hot.astype(BF16), before.astype(BF16))
    block_rank = jnp.sum(earlier * owner_hot, axis=0, keepdims=True)
    block_slot = jnp.broadcast_to(owner.astype(F32) * most + block_rank, (8, n_blocks))
    widen = (iota((n_blocks, ff), 1) // PUSH_ROWS == iota((n_blocks, ff), 0)).astype(F32)
    key = mm(block_slot.astype(BF16), widen.astype(BF16))[0:1].astype(I32)
    key = key * PUSH_ROWS + iota((1, ff), 1) % PUSH_ROWS
    big[...] = (iota((nz * most * PUSH_ROWS, ff), 0) == key).astype(F32).astype(BF16)

    pl.semaphore_wait(barrier, nz - 1 + 3 + 2)

    pend_copy = remote(pend, inc, pend_sem.at[0], pend_sem.at[1], section=prev_sec)
    pend_copy.start()

    def first_copy(d):
        other = lax.rem(e + d, EXPERTS)
        return remote(hsend.at[a, other], hbuf.at[a, b, m, e % 2], ha_s.at[d], ha_r.at[e % 2],
                      expert=other * grp + m)

    own_hidden = pltpu.make_async_copy(hsend.at[a, e], hbuf.at[a, b, m, e % 2], own_sem.at[0])

    @pl.when(b == e // 2)
    def _():
        for d in range(1, EXPERTS):
            first_copy(d).start()
        own_hidden.start()

    pend_copy.wait_recv()
    rows = mm(placing, inc[...])
    rid_rows = iota((cp, LANES), 0)
    for x in range(EXPERTS):
        for j in range(grp):
            piece = rows[x * cp:(x + 1) * cp, j * LANES:(j + 1) * LANES]
            rsend[x * grp + j] = jnp.where(rid_rows >= gate_row, gate_rows[x], piece).astype(BF16)

    def row_copy(k):
        dest = lax.rem(z + k, nz)
        return remote(rsend.at[dest], rbuf.at[here], rs.at[k], rr.at[here], expert=dest)

    def row_arrival(k):
        src = lax.rem(z + k, nz)
        return remote(rsend.at[src], rbuf.at[place(src)], rs.at[k], rr.at[place(src)], expert=src)

    def row_pair(i):
        k = nz // 2 - i
        row_copy(k).start()

        @pl.when(k < nz // 2)
        def _():
            row_copy(nz - k).start()

    per_step = nz // 2 // grp

    @pl.loop(0, per_step)
    def _(i):
        row_pair(i)

    own_rows = pltpu.make_async_copy(rsend.at[z], rbuf.at[here], own_sem.at[1])
    own_rows.start()

    def chain_copy(block, way):
        return remote(hbuf.at[a, b, block], hbuf.at[a, b, block], zs.at[way, block], zr.at[block],
                      expert=lax.rem(z + (1 if way == 0 else nz - 1), nz))

    def x_copy(block, h):
        return remote(hbuf.at[h, b, block], hbuf.at[h, b, block], xs.at[block], xr.at[block],
                      copy=(1 - a) * 2 + b)

    def core_copy(block, h, kind, core):
        return remote(hbuf.at[h, core, block], hbuf.at[h, core, block], cs.at[kind, block],
                      cr.at[kind, block], copy=a * 2 + 1 - b)

    for i in range(2):
        @pl.when(2 * b + i != e)
        def _():
            remote(hsend.at[a, 0], hbuf.at[a, b, m, i], ha_s.at[0], ha_r.at[i], expert=m).wait_recv()

    @pl.when(b == e // 2)
    def _():
        own_hidden.wait()

    def spread(block):
        x_copy(block, a).start()
        core_copy(block, a, 0, b).start()

    @pl.when(m < grp - 1)
    def _():
        chain_copy(m, 0).start()

    @pl.when(m > 0)
    def _():
        chain_copy(m, 1).start()

    spread(m)

    @pl.loop(1, grp)
    def _(k):
        @pl.when(m - k >= 0)
        def _():
            chain_copy(m - k, 0).wait_recv()

            @pl.when(m < grp - 1)
            def _():
                chain_copy(m - k, 0).start()

            spread(m - k)

        @pl.when(m + k < grp)
        def _():
            chain_copy(m + k, 1).wait_recv()

            @pl.when(m > 0)
            def _():
                chain_copy(m + k, 1).start()

            spread(m + k)

        for i in range(per_step):
            row_pair(k * per_step + i)

    @pl.loop(0, grp)
    def _(block):
        x_copy(block, 1 - a).wait_recv()
        core_copy(block, 1 - a, 1, b).start()

    for load in loads:
        load.wait()

    @pl.loop(0, grp)
    def _(block):
        core_copy(block, a, 0, 1 - b).wait_recv()
        core_copy(block, 1 - a, 1, 1 - b).wait_recv()

    def flat(blocks):
        return blocks.astype(F32).reshape(nz * cp, blocks.shape[-1])

    for h in range(2):
        hflat[h] = flat(hbuf[h]).astype(BF16)
    outs[...] = mm(hflat[0], wv[0:half, :]) + mm(hflat[1], wv[half:ff, :])

    own_rows.wait()

    @pl.loop(1, nz)
    def _(k):
        row_arrival(k).wait_recv()

    gates[...] = jnp.zeros(gates.shape, F32)
    for p in range(nz):
        gates[p:p + 1, :] = rbuf[p].astype(F32)[gate_row:gate_row + 1]
    gate_cols = gates[...].T
    for p in range(nz):
        scaled[p] = gate_cols[0:cp, p:p + 1] * rbuf[p].astype(F32)
    scaled_all = scaled[...].reshape(nz * cp, LANES).astype(BF16)
    for h in range(2):
        grad = mm(scaled_all, hflat[h], ((0,), (0,))).T
        rows_h = pl.ds(h * half, half)
        first = beta_first * m1v[rows_h, :] + (1.0 - beta_first) * grad
        second = beta_second * m2v[rows_h, :] + (1.0 - beta_second) * grad * grad
        update = first / bias_first / (jnp.sqrt(second / bias_second) + adam_eps) + decay_rate * mav[rows_h, :]
        new = mav[rows_h, :] - learn_rate * update
        m1v[rows_h, :] = first
        m2v[rows_h, :] = second
        mav[rows_h, :] = new
        fresh[rows_h, :] = new.astype(BF16)
    per_owner = most * PUSH_ROWS
    for x in range(EXPERTS):
        part = mm(big[x * grp * per_owner:(x + 1) * grp * per_owner, :], fresh[...])
        for j in range(grp):
            psend[x * grp + j] = part[j * per_owner:(j + 1) * per_owner].astype(BF16)

    def push_copy(k):
        dest = lax.rem(z + k, nz)
        return remote(psend.at[dest], serv.at[z], ps.at[k], pr.at[z], expert=dest)

    def push_arrival(k):
        src = lax.rem(z + k, nz)
        return remote(psend.at[src], serv.at[src], ps.at[k], pr.at[src], expert=src)

    def push_pair(i):
        k = nz // 2 - i
        push_copy(k).start()

        @pl.when(k < nz // 2)
        def _():
            push_copy(nz - k).start()

    early = nz // 8

    @pl.loop(0, early)
    def _(i):
        push_pair(i)

    product = outs[...] * flat(rbuf[...])
    shares = mm(jnp.ones((8, LANES), F32), product, ((1,), (1,)), HIGHEST)
    for p in range(nz):
        ret_s[p, :, 0:cp] = shares[0:1, p * cp:(p + 1) * cp]

    def ret_copy(k):
        dest = lax.rem(z + k, nz)
        return remote(ret_s.at[place(dest)], ret_r.at[z], gs.at[k], gr.at[z], expert=dest)

    def ret_arrival(k):
        src = lax.rem(z + k, nz)
        return remote(ret_s.at[src], ret_r.at[src], gs.at[k], gr.at[src], expert=src)

    @pl.loop(0, nz // 2)
    def _(i):
        k = nz // 2 - i
        ret_copy(k).start()

        @pl.when(k < nz // 2)
        def _():
            ret_copy(nz - k).start()

    @pl.loop(early, nz // 2)
    def _(i):
        push_pair(i)

    own_push = pltpu.make_async_copy(psend.at[z], serv.at[z], own_sem.at[2])
    own_push.start()
    stores = [
        pltpu.make_async_copy(src, dst, st_sem.at[i])
        for i, (src, dst) in enumerate(((m1v, m1_out), (m2v, m2_out), (mav, ma_out)))
    ]
    for store in stores:
        store.start()

    own_ret = pltpu.make_async_copy(ret_s.at[here], ret_r.at[z], own_sem.at[3])
    own_ret.start()
    own_ret.wait()

    @pl.loop(1, nz)
    def _(k):
        ret_arrival(k).wait_recv()

    for x in range(EXPERTS):
        total = ret_r[x * grp]
        for j in range(1, grp):
            total = total + ret_r[x * grp + j]
        cp_s[x:x + 1, :] = total

    def share_copy(k):
        return remote(cp_s, cp_r.at[k], ks.at[k], kr.at[k], copy=lax.rem(c + k, 4))

    for k in range(1, 4):
        share_copy(k).start()
    for k in range(1, 4):
        share_copy(k).wait_recv()
    whole = cp_s[...] + cp_r[1] + cp_r[2] + cp_r[3]
    whole = jnp.where(iota(whole.shape, 1) < cp, whole, 0.0)
    gate_grad = jnp.zeros((8, tok), F32)
    for x in range(EXPERTS):
        gate_grad += mm(jnp.broadcast_to(whole[x:x + 1], (8, LANES)), by_rank[x], precision=HIGHEST)
    logit_grad = (gate_grad[0:1] * gate) * (onehot - prob)
    gates[0:EXPERTS, :] = logit_grad
    grad_cols = gates[...].T
    term = inc[...].astype(F32)
    extra = grad_cols[:, 0:1] * rw_t[0:1, :]
    for x in range(1, EXPERTS):
        extra += grad_cols[:, x:x + 1] * rw_t[x:x + 1, :]
    inc[...] = (term + extra).astype(BF16)
    stores.append(pltpu.make_async_copy(inc, ig_out, st_sem.at[3]))
    stores[3].start()

    pend_copy.wait_send()
    for k in range(1, 4):
        share_copy(k).wait_send()

    @pl.when(b == e // 2)
    def _():
        for d in range(1, EXPERTS):
            first_copy(d).wait_send()

    @pl.loop(0, grp)
    def _(block):
        @pl.when((block <= m) & (m < grp - 1))
        def _():
            chain_copy(block, 0).wait_send()

        @pl.when((block >= m) & (m > 0))
        def _():
            chain_copy(block, 1).wait_send()

        x_copy(block, a).wait_send()
        core_copy(block, a, 0, b).wait_send()
        core_copy(block, 1 - a, 1, b).wait_send()

    @pl.loop(1, nz)
    def _(k):
        row_copy(k).wait_send()
        ret_copy(k).wait_send()

    for store in stores:
        store.wait()
    own_push.wait()

    @pl.loop(1, nz)
    def _(k):
        push_copy(k).wait_send()
        push_arrival(k).wait_recv()


def hand_over(n, *refs):
    sources, dests, held, sems = refs[:n], refs[n:2 * n], refs[2 * n:3 * n], refs[3 * n]
    fetches = [pltpu.make_async_copy(sources[i], held[i], sems.at[0, i]) for i in range(n)]
    stores = [pltpu.make_async_copy(held[i], dests[i], sems.at[1, i]) for i in range(n)]
    for fetch in fetches:
        fetch.start()
    for fetch, store in zip(fetches, stores):
        fetch.wait()
        store.start()
    for store in stores:
        store.wait()


def per_device(
    pending, hidden, logits, routes, router_weight, down_weight, master, moment_first, moment_second, push_plan,
):
    n_sec, nz = lax.axis_size("section"), lax.axis_size("expert")
    tok, width = pending.shape[1:]
    ff = hidden.shape[2]
    grp = nz // EXPERTS
    capacity = tok * 9 // (EXPERTS * 8)
    cp = 40
    gate_row = 36
    n_blocks = ff // PUSH_ROWS
    most = max(2, (3 * n_blocks + 2 * nz - 1) // (2 * nz))
    assert capacity <= gate_row and width == grp * LANES and tok == LANES
    per_owner = most * PUSH_ROWS
    half = ff // 2
    vmem, hbm = pl.BlockSpec(memory_space=pltpu.VMEM), pl.BlockSpec(memory_space=pl.ANY)
    dma = pltpu.SemaphoreType.DMA
    piece = jax.ShapeDtypeStruct((ff, LANES), F32)
    results = pl.pallas_call(
        functools.partial(kernel, n_sec, nz, cp, gate_row),
        out_shape=(
            jax.ShapeDtypeStruct((tok, width), BF16), piece, piece, piece,
            jax.ShapeDtypeStruct((nz, per_owner, LANES), BF16),
        ),
        in_specs=[hbm] + [vmem] * 4 + [hbm] * 4 + [vmem],
        out_specs=[hbm] * 5,
        scratch_shapes=[
            pltpu.VMEM((tok, width), BF16),
            pltpu.VMEM((2, EXPERTS, cp, half), BF16),
            pltpu.VMEM((2, 2, grp, 2, cp, half), BF16),
            pltpu.VMEM((2, nz * cp, half), BF16),
            pltpu.VMEM((nz * cp, LANES), F32),
            pltpu.VMEM((nz, cp, LANES), BF16),
            pltpu.VMEM((nz, cp, LANES), BF16),
            pltpu.VMEM((nz, cp, LANES), F32),
            pltpu.VMEM((LANES, LANES), F32),
            pltpu.VMEM((nz * per_owner, ff), BF16),
            pltpu.VMEM((nz, per_owner, LANES), BF16),
            pltpu.VMEM((nz, 1, LANES), F32),
            pltpu.VMEM((nz, 1, LANES), F32),
            pltpu.VMEM((EXPERTS, LANES), F32),
            pltpu.VMEM((4, EXPERTS, LANES), F32),
            pltpu.VMEM((ff, LANES), BF16),
            pltpu.VMEM((ff, LANES), F32),
            pltpu.VMEM((ff, LANES), F32),
            pltpu.VMEM((ff, LANES), F32),
            pltpu.VMEM((ff, LANES), BF16),
            dma((4,)), dma((4,)), dma((2,)), dma((4,)),
            dma((EXPERTS,)), dma((2,)),
            dma((2, grp)), dma((grp,)),
            dma((grp,)), dma((grp,)),
            dma((2, grp)), dma((2, grp)),
            dma((nz,)), dma((nz,)),
            dma((nz,)), dma((nz,)),
            dma((nz,)), dma((nz,)),
            dma((4,)), dma((4,)),
        ],
        compiler_params=pltpu.CompilerParams(
            collective_id=0, has_side_effects=True, vmem_limit_bytes=63 * 1024 * 1024
        ),
        cost_estimate=pl.CostEstimate(flops=10**9, bytes_accessed=8 * 10**6, transcendentals=10**5),
    )(
        pending[0], hidden[0], logits[0].T, routes[0].T, router_weight[0].T,
        down_weight[0, 0], master[0, 0], moment_first[0, 0], moment_second[0, 0], push_plan[0, 0, 0].T,
    )
    n = len(results)
    input_grad, fresh_master, first, second, serving = pl.pallas_call(
        functools.partial(hand_over, n),
        out_shape=tuple(jax.ShapeDtypeStruct(r.shape, r.dtype) for r in results),
        in_specs=[hbm] * n,
        out_specs=[hbm] * n,
        scratch_shapes=[pltpu.VMEM(r.shape, r.dtype) for r in results] + [dma((2, n))],
        compiler_params=pltpu.CompilerParams(vmem_limit_bytes=63 * 1024 * 1024),
        cost_estimate=pl.CostEstimate(flops=0, bytes_accessed=4 * 10**6, transcendentals=0),
    )(*results)
    return (
        input_grad[None],
        fresh_master[None, None],
        first[None, None],
        second[None, None],
        serving.reshape(nz * most, PUSH_ROWS, LANES)[None, None, None],
    )


def solution(mesh):
    return jax.shard_map(
        per_device,
        mesh=mesh,
        in_specs=(
            P("section", "expert", "copy"),
            P("section", "expert", None),
            P("section", "expert", None),
            P("section", "expert", None),
            P("section", "copy", None),
            P("section", "copy", None, "expert"),
            P("section", "copy", None, "expert"),
            P("section", "copy", None, "expert"),
            P("section", "copy", None, "expert"),
            P("section", "copy", "expert", None, None),
        ),
        out_specs=(
            P("section", "expert", "copy"),
            P("section", "copy", None, "expert"),
            P("section", "copy", None, "expert"),
            P("section", "copy", None, "expert"),
            P("section", "copy", "expert", None, None, None),
        ),
        check_vma=False,
    )
```

```python
import functools

import jax
import jax.numpy as jnp
from jax import lax
from jax.experimental import pallas as pl
from jax.experimental.pallas import tpu as pltpu
from jax.sharding import PartitionSpec as P

PUSH_ROWS = 8
EXPERTS = 4
PARTS = 4
LANES = 128

beta_first = 0.9
beta_second = 0.95
learn_rate = 0.002
decay_rate = 0.1
adam_eps = 1e-08
bias_first = 1.0 - 0.9**10
bias_second = 1.0 - 0.95**10

F32 = jnp.float32
BF16 = jnp.bfloat16
I32 = jnp.int32
HIGHEST = lax.Precision.HIGHEST


def iota(shape, dim):
    return lax.broadcasted_iota(I32, shape, dim)


def mm(x, y, dims=((1,), (0,)), precision=None):
    return lax.dot_general(x, y, (dims, ((), ())), precision=precision, preferred_element_type=F32)


def kernel(
    n_sec, nz, slot_rows, gate_row,
    pend, hid, log_t, route_t, rw_t, w_hbm, ma_hbm, m1_hbm, m2_hbm, plan,
    ig_out, ma_out, m1_out, m2_out, serv,
    inc, hsend, hbuf, hflat, outs, rsend, rbuf, scaled, gates, big, psend, ret_s, ret_r, cp_s, cp_r,
    wv, mav, m1v, m2v, fresh,
    ld_sem, st_sem, pend_sem, own_sem, ha_s, ha_r, zs, zr, xs, xr, cs, cr, rs, rr, ps, pr, gs, gr, ks, kr,
):
    grp = nz // EXPERTS
    cp = slot_rows
    tok = hid.shape[0]
    half = hid.shape[1] // 2
    ff = 2 * half
    s, z, c = lax.axis_index("section"), lax.axis_index("expert"), lax.axis_index("copy")
    a, b = c // 2, c % 2
    e, m = z // grp, z % grp
    here = (e // 2) * (2 * grp) + m * 2 + e % 2

    def place(p):
        q = p // grp
        return (q // 2) * (2 * grp) + (p % grp) * 2 + q % 2

    def remote(src, dst, send, recv, **axis):
        return pltpu.make_async_remote_copy(
            src_ref=src, dst_ref=dst, send_sem=send, recv_sem=recv,
            device_id=axis, device_id_type=pl.DeviceIdType.MESH,
        )

    loads = [
        pltpu.make_async_copy(src, dst, ld_sem.at[i])
        for i, (src, dst) in enumerate(((w_hbm, wv), (m1_hbm, m1v), (m2_hbm, m2v), (ma_hbm, mav)))
    ]
    for load in loads:
        load.start()

    barrier = pltpu.get_barrier_semaphore()
    prev_sec, next_sec = lax.rem(s + n_sec - 1, n_sec), lax.rem(s + 1, n_sec)

    def greet(**axis):
        pl.semaphore_signal(barrier, inc=1, device_id=axis, device_id_type=pl.DeviceIdType.MESH)

    @pl.loop(0, nz // 2)
    def _(i):
        k = nz // 2 - i
        greet(expert=lax.rem(z + k, nz))

        @pl.when(k < nz // 2)
        def _():
            greet(expert=lax.rem(z + nz - k, nz))

    greet(section=prev_sec)
    greet(section=next_sec)
    for k in range(1, 4):
        greet(copy=lax.rem(c + k, 4))

    logit = log_t[...]
    expd = jnp.exp(logit - jnp.max(logit, axis=0, keepdims=True))
    prob = expd / jnp.sum(expd, axis=0, keepdims=True)
    rid = route_t[...]
    onehot = (iota((EXPERTS, tok), 0) == rid).astype(F32)
    gate = jnp.sum(prob * onehot, axis=0, keepdims=True)
    hot8 = (iota((8, tok), 0) == rid).astype(F32)
    upper = (iota((tok, tok), 0) <= iota((tok, tok), 1)).astype(F32)
    running = mm(hot8.astype(BF16), upper.astype(BF16))
    rank = jnp.sum(running * hot8, axis=0, keepdims=True).astype(I32) - 1
    slot = rid * cp + rank
    placing = (iota((EXPERTS * cp, tok), 0) == slot).astype(F32).astype(BF16)
    gate8 = jnp.broadcast_to(gate, (8, tok)).astype(BF16)
    by_rank = []
    for x in range(EXPERTS):
        rank_x = jnp.where(rid == x, rank, -1)
        by_rank.append((iota((LANES, tok), 0) == rank_x).astype(F32))

    packed = mm(placing, hid[...])
    for x in range(EXPERTS):
        for h in range(2):
            hsend[h, x] = packed[x * cp:(x + 1) * cp, h * half:(h + 1) * half].astype(BF16)

    gate_rows = [
        mm(gate8, by_rank[x].astype(BF16), ((1,), (1,)))[0:1] for x in range(EXPERTS)
    ]

    n_blocks = plan.shape[1]
    most = psend.shape[1] // PUSH_ROWS
    owner = plan[...]
    owner_hot = (iota((nz, n_blocks), 0) == owner).astype(F32)
    before = (iota((n_blocks, n_blocks), 0) < iota((n_blocks, n_blocks), 1)).astype(F32)
    earlier = mm(owner_hot.astype(BF16), before.astype(BF16))
    block_rank = jnp.sum(earlier * owner_hot, axis=0, keepdims=True)
    block_slot = jnp.broadcast_to(owner.astype(F32) * most + block_rank, (8, n_blocks))
    widen = (iota((n_blocks, ff), 1) // PUSH_ROWS == iota((n_blocks, ff), 0)).astype(F32)
    key = mm(block_slot.astype(BF16), widen.astype(BF16))[0:1].astype(I32)
    key = key * PUSH_ROWS + iota((1, ff), 1) % PUSH_ROWS
    big[...] = (iota((nz * most * PUSH_ROWS, ff), 0) == key).astype(F32).astype(BF16)

    pl.semaphore_wait(barrier, nz - 1 + 3 + 2)

    pend_copy = remote(pend, inc, pend_sem.at[0], pend_sem.at[1], section=prev_sec)
    pend_copy.start()

    def first_copy(d):
        other = lax.rem(e + d, EXPERTS)
        return remote(hsend.at[a, other], hbuf.at[a, b, m, e % 2], ha_s.at[d], ha_r.at[e % 2],
                      expert=other * grp + m)

    own_hidden = pltpu.make_async_copy(hsend.at[a, e], hbuf.at[a, b, m, e % 2], own_sem.at[0])

    @pl.when(b == e // 2)
    def _():
        for d in range(1, EXPERTS):
            first_copy(d).start()
        own_hidden.start()

    pend_copy.wait_recv()
    rows = mm(placing, inc[...])
    rid_rows = iota((cp, LANES), 0)
    for x in range(EXPERTS):
        for j in range(grp):
            piece = rows[x * cp:(x + 1) * cp, j * LANES:(j + 1) * LANES]
            rsend[x * grp + j] = jnp.where(rid_rows >= gate_row, gate_rows[x], piece).astype(BF16)

    def row_copy(k):
        dest = lax.rem(z + k, nz)
        return remote(rsend.at[dest], rbuf.at[here], rs.at[k], rr.at[here], expert=dest)

    def row_arrival(k):
        src = lax.rem(z + k, nz)
        return remote(rsend.at[src], rbuf.at[place(src)], rs.at[k], rr.at[place(src)], expert=src)

    def row_pair(i):
        k = nz // 2 - i
        row_copy(k).start()

        @pl.when(k < nz // 2)
        def _():
            row_copy(nz - k).start()

    per_step = nz // 2 // grp

    @pl.loop(0, per_step)
    def _(i):
        row_pair(i)

    own_rows = pltpu.make_async_copy(rsend.at[z], rbuf.at[here], own_sem.at[1])
    own_rows.start()

    def chain_copy(block, way):
        return remote(hbuf.at[a, b, block], hbuf.at[a, b, block], zs.at[way, block], zr.at[block],
                      expert=lax.rem(z + (1 if way == 0 else nz - 1), nz))

    def x_copy(block, h):
        return remote(hbuf.at[h, b, block], hbuf.at[h, b, block], xs.at[block], xr.at[block],
                      copy=(1 - a) * 2 + b)

    def core_copy(block, h, kind, core):
        return remote(hbuf.at[h, core, block], hbuf.at[h, core, block], cs.at[kind, block],
                      cr.at[kind, block], copy=a * 2 + 1 - b)

    for i in range(2):
        @pl.when(2 * b + i != e)
        def _():
            remote(hsend.at[a, 0], hbuf.at[a, b, m, i], ha_s.at[0], ha_r.at[i], expert=m).wait_recv()

    @pl.when(b == e // 2)
    def _():
        own_hidden.wait()

    def spread(block):
        x_copy(block, a).start()
        core_copy(block, a, 0, b).start()

    @pl.when(m < grp - 1)
    def _():
        chain_copy(m, 0).start()

    @pl.when(m > 0)
    def _():
        chain_copy(m, 1).start()

    spread(m)

    @pl.loop(1, grp)
    def _(k):
        @pl.when(m - k >= 0)
        def _():
            chain_copy(m - k, 0).wait_recv()

            @pl.when(m < grp - 1)
            def _():
                chain_copy(m - k, 0).start()

            spread(m - k)

        @pl.when(m + k < grp)
        def _():
            chain_copy(m + k, 1).wait_recv()

            @pl.when(m > 0)
            def _():
                chain_copy(m + k, 1).start()

            spread(m + k)

        for i in range(per_step):
            row_pair(k * per_step + i)

    @pl.loop(0, grp)
    def _(block):
        x_copy(block, 1 - a).wait_recv()
        core_copy(block, 1 - a, 1, b).start()

    for load in loads:
        load.wait()

    @pl.loop(0, grp)
    def _(block):
        core_copy(block, a, 0, 1 - b).wait_recv()
        core_copy(block, 1 - a, 1, 1 - b).wait_recv()

    def flat(blocks):
        return blocks.astype(F32).reshape(nz * cp, blocks.shape[-1])

    for h in range(2):
        hflat[h] = flat(hbuf[h]).astype(BF16)
    outs[...] = mm(hflat[0], wv[0:half, :]) + mm(hflat[1], wv[half:ff, :])

    own_rows.wait()

    @pl.loop(1, nz)
    def _(k):
        row_arrival(k).wait_recv()

    gates[...] = jnp.zeros(gates.shape, F32)
    for p in range(nz):
        gates[p:p + 1, :] = rbuf[p].astype(F32)[gate_row:gate_row + 1]
    gate_cols = gates[...].T
    for p in range(nz):
        scaled[p] = gate_cols[0:cp, p:p + 1] * rbuf[p].astype(F32)
    scaled_all = scaled[...].reshape(nz * cp, LANES).astype(BF16)
    for h in range(2):
        grad = mm(scaled_all, hflat[h], ((0,), (0,))).T
        rows_h = pl.ds(h * half, half)
        first = beta_first * m1v[rows_h, :] + (1.0 - beta_first) * grad
        second = beta_second * m2v[rows_h, :] + (1.0 - beta_second) * grad * grad
        update = first / bias_first / (jnp.sqrt(second / bias_second) + adam_eps) + decay_rate * mav[rows_h, :]
        new = mav[rows_h, :] - learn_rate * update
        m1v[rows_h, :] = first
        m2v[rows_h, :] = second
        mav[rows_h, :] = new
        fresh[rows_h, :] = new.astype(BF16)
    per_owner = most * PUSH_ROWS
    for x in range(EXPERTS):
        part = mm(big[x * grp * per_owner:(x + 1) * grp * per_owner, :], fresh[...])
        for j in range(grp):
            psend[x * grp + j] = part[j * per_owner:(j + 1) * per_owner].astype(BF16)

    def push_copy(k):
        dest = lax.rem(z + k, nz)
        return remote(psend.at[dest], serv.at[z], ps.at[k], pr.at[z], expert=dest)

    def push_arrival(k):
        src = lax.rem(z + k, nz)
        return remote(psend.at[src], serv.at[src], ps.at[k], pr.at[src], expert=src)

    def push_pair(i):
        k = nz // 2 - i
        push_copy(k).start()

        @pl.when(k < nz // 2)
        def _():
            push_copy(nz - k).start()

    early = nz // 8

    @pl.loop(0, early)
    def _(i):
        push_pair(i)

    product = outs[...] * flat(rbuf[...])
    shares = mm(jnp.ones((8, LANES), F32), product, ((1,), (1,)), HIGHEST)
    for p in range(nz):
        ret_s[p, :, 0:cp] = shares[0:1, p * cp:(p + 1) * cp]

    def ret_copy(k):
        dest = lax.rem(z + k, nz)
        return remote(ret_s.at[place(dest)], ret_r.at[z], gs.at[k], gr.at[z], expert=dest)

    def ret_arrival(k):
        src = lax.rem(z + k, nz)
        return remote(ret_s.at[src], ret_r.at[src], gs.at[k], gr.at[src], expert=src)

    @pl.loop(0, nz // 2)
    def _(i):
        k = nz // 2 - i
        ret_copy(k).start()

        @pl.when(k < nz // 2)
        def _():
            ret_copy(nz - k).start()

    @pl.loop(early, nz // 2)
    def _(i):
        push_pair(i)

    own_push = pltpu.make_async_copy(psend.at[z], serv.at[z], own_sem.at[2])
    own_push.start()
    stores = [
        pltpu.make_async_copy(src, dst, st_sem.at[i])
        for i, (src, dst) in enumerate(((m1v, m1_out), (m2v, m2_out), (mav, ma_out)))
    ]
    for store in stores:
        store.start()

    own_ret = pltpu.make_async_copy(ret_s.at[here], ret_r.at[z], own_sem.at[3])
    own_ret.start()
    own_ret.wait()

    @pl.loop(1, nz)
    def _(k):
        ret_arrival(k).wait_recv()

    for x in range(EXPERTS):
        total = ret_r[x * grp]
        for j in range(1, grp):
            total = total + ret_r[x * grp + j]
        cp_s[x:x + 1, :] = total

    def share_copy(k):
        return remote(cp_s, cp_r.at[k], ks.at[k], kr.at[k], copy=lax.rem(c + k, 4))

    for k in range(1, 4):
        share_copy(k).start()
    for k in range(1, 4):
        share_copy(k).wait_recv()
    whole = cp_s[...] + cp_r[1] + cp_r[2] + cp_r[3]
    whole = jnp.where(iota(whole.shape, 1) < cp, whole, 0.0)
    gate_grad = jnp.zeros((8, tok), F32)
    for x in range(EXPERTS):
        gate_grad += mm(jnp.broadcast_to(whole[x:x + 1], (8, LANES)), by_rank[x], precision=HIGHEST)
    logit_grad = (gate_grad[0:1] * gate) * (onehot - prob)
    gates[0:EXPERTS, :] = logit_grad
    grad_cols = gates[...].T
    term = inc[...].astype(F32)
    extra = grad_cols[:, 0:1] * rw_t[0:1, :]
    for x in range(1, EXPERTS):
        extra += grad_cols[:, x:x + 1] * rw_t[x:x + 1, :]
    inc[...] = (term + extra).astype(BF16)
    stores.append(pltpu.make_async_copy(inc, ig_out, st_sem.at[3]))
    stores[3].start()

    pend_copy.wait_send()
    for k in range(1, 4):
        share_copy(k).wait_send()

    @pl.when(b == e // 2)
    def _():
        for d in range(1, EXPERTS):
            first_copy(d).wait_send()

    @pl.loop(0, grp)
    def _(block):
        @pl.when((block <= m) & (m < grp - 1))
        def _():
            chain_copy(block, 0).wait_send()

        @pl.when((block >= m) & (m > 0))
        def _():
            chain_copy(block, 1).wait_send()

        x_copy(block, a).wait_send()
        core_copy(block, a, 0, b).wait_send()
        core_copy(block, 1 - a, 1, b).wait_send()

    @pl.loop(1, nz)
    def _(k):
        row_copy(k).wait_send()
        ret_copy(k).wait_send()

    for store in stores:
        store.wait()
    own_push.wait()

    @pl.loop(1, nz)
    def _(k):
        push_copy(k).wait_send()
        push_arrival(k).wait_recv()


def hand_over(n, *refs):
    sources, dests, held, sems = refs[:n], refs[n:2 * n], refs[2 * n:3 * n], refs[3 * n]
    fetches, stores = [], []
    for i in range(n):
        rows = held[i].shape[0] // PARTS
        for q in range(PARTS):
            part = pl.ds(q * rows, rows)
            k = i * PARTS + q
            fetches.append(pltpu.make_async_copy(sources[i].at[part], held[i].at[part], sems.at[0, k]))
            stores.append(pltpu.make_async_copy(held[i].at[part], dests[i].at[part], sems.at[1, k]))
    for fetch in fetches:
        fetch.start()
    for fetch, store in zip(fetches, stores):
        fetch.wait()
        store.start()
    for store in stores:
        store.wait()


def per_device(
    pending, hidden, logits, routes, router_weight, down_weight, master, moment_first, moment_second, push_plan,
):
    n_sec, nz = lax.axis_size("section"), lax.axis_size("expert")
    tok, width = pending.shape[1:]
    ff = hidden.shape[2]
    grp = nz // EXPERTS
    capacity = tok * 9 // (EXPERTS * 8)
    cp = 40
    gate_row = 36
    n_blocks = ff // PUSH_ROWS
    most = max(2, (3 * n_blocks + 2 * nz - 1) // (2 * nz))
    assert capacity <= gate_row and width == grp * LANES and tok == LANES
    per_owner = most * PUSH_ROWS
    half = ff // 2
    vmem, hbm = pl.BlockSpec(memory_space=pltpu.VMEM), pl.BlockSpec(memory_space=pl.ANY)
    dma = pltpu.SemaphoreType.DMA
    piece = jax.ShapeDtypeStruct((ff, LANES), F32)
    results = pl.pallas_call(
        functools.partial(kernel, n_sec, nz, cp, gate_row),
        out_shape=(
            jax.ShapeDtypeStruct((tok, width), BF16), piece, piece, piece,
            jax.ShapeDtypeStruct((nz, per_owner, LANES), BF16),
        ),
        in_specs=[hbm] + [vmem] * 4 + [hbm] * 4 + [vmem],
        out_specs=[hbm] * 5,
        scratch_shapes=[
            pltpu.VMEM((tok, width), BF16),
            pltpu.VMEM((2, EXPERTS, cp, half), BF16),
            pltpu.VMEM((2, 2, grp, 2, cp, half), BF16),
            pltpu.VMEM((2, nz * cp, half), BF16),
            pltpu.VMEM((nz * cp, LANES), F32),
            pltpu.VMEM((nz, cp, LANES), BF16),
            pltpu.VMEM((nz, cp, LANES), BF16),
            pltpu.VMEM((nz, cp, LANES), F32),
            pltpu.VMEM((LANES, LANES), F32),
            pltpu.VMEM((nz * per_owner, ff), BF16),
            pltpu.VMEM((nz, per_owner, LANES), BF16),
            pltpu.VMEM((nz, 1, LANES), F32),
            pltpu.VMEM((nz, 1, LANES), F32),
            pltpu.VMEM((EXPERTS, LANES), F32),
            pltpu.VMEM((4, EXPERTS, LANES), F32),
            pltpu.VMEM((ff, LANES), BF16),
            pltpu.VMEM((ff, LANES), F32),
            pltpu.VMEM((ff, LANES), F32),
            pltpu.VMEM((ff, LANES), F32),
            pltpu.VMEM((ff, LANES), BF16),
            dma((4,)), dma((4,)), dma((2,)), dma((4,)),
            dma((EXPERTS,)), dma((2,)),
            dma((2, grp)), dma((grp,)),
            dma((grp,)), dma((grp,)),
            dma((2, grp)), dma((2, grp)),
            dma((nz,)), dma((nz,)),
            dma((nz,)), dma((nz,)),
            dma((nz,)), dma((nz,)),
            dma((4,)), dma((4,)),
        ],
        compiler_params=pltpu.CompilerParams(
            collective_id=0, has_side_effects=True, vmem_limit_bytes=63 * 1024 * 1024
        ),
        cost_estimate=pl.CostEstimate(flops=10**9, bytes_accessed=8 * 10**6, transcendentals=10**5),
    )(
        pending[0], hidden[0], logits[0].T, routes[0].T, router_weight[0].T,
        down_weight[0, 0], master[0, 0], moment_first[0, 0], moment_second[0, 0], push_plan[0, 0, 0].T,
    )
    n = len(results)
    input_grad, fresh_master, first, second, serving = pl.pallas_call(
        functools.partial(hand_over, n),
        out_shape=tuple(jax.ShapeDtypeStruct(r.shape, r.dtype) for r in results),
        in_specs=[hbm] * n,
        out_specs=[hbm] * n,
        scratch_shapes=[pltpu.VMEM(r.shape, r.dtype) for r in results] + [dma((2, n * PARTS))],
        compiler_params=pltpu.CompilerParams(vmem_limit_bytes=63 * 1024 * 1024),
        cost_estimate=pl.CostEstimate(flops=0, bytes_accessed=4 * 10**6, transcendentals=0),
    )(*results)
    return (
        input_grad[None],
        fresh_master[None, None],
        first[None, None],
        second[None, None],
        serving.reshape(nz * most, PUSH_ROWS, LANES)[None, None, None],
    )


def solution(mesh):
    return jax.shard_map(
        per_device,
        mesh=mesh,
        in_specs=(
            P("section", "expert", "copy"),
            P("section", "expert", None),
            P("section", "expert", None),
            P("section", "expert", None),
            P("section", "copy", None),
            P("section", "copy", None, "expert"),
            P("section", "copy", None, "expert"),
            P("section", "copy", None, "expert"),
            P("section", "copy", None, "expert"),
            P("section", "copy", "expert", None, None),
        ),
        out_specs=(
            P("section", "expert", "copy"),
            P("section", "copy", None, "expert"),
            P("section", "copy", None, "expert"),
            P("section", "copy", None, "expert"),
            P("section", "copy", "expert", None, None, None),
        ),
        check_vma=False,
    )
```
